512 devices in a mesh: tm: 32 (over y_lo, z), tok: 16 (over y_hi, x, core).
Axes of the slice: x: 4, y: 8 (y_hi: 2, y_lo: 4; y = y_hi * 4 + y_lo), z: 8, core: 2. Of those that a mesh axis runs over, the one named last changes fastest.
Arguments:
- hidden_states: bfloat16 [32, 1024, 1280], P('tm', 'tok'), may hold values from -6 to 6
- norm_gain: float32 [1280], replicated, may hold values from 0.1 to 1.9
- norm_bias: float32 [1280], replicated, may hold values from -3 to 3
- q_weight: bfloat16 [1280, 1024], P(None, 'tok'), may hold values from -0.5 to 0.5
- k_weight: bfloat16 [1280, 1024], P(None, 'tok'), may hold values from -0.25 to 0.25
- v_weight: bfloat16 [1280, 1024], P(None, 'tok'), may hold values from -0.15625 to 0.15625
- out_weight: bfloat16 [1024, 1280], P('tok'), may hold values from -0.75 to 0.75
Outputs:
- attended_out: bfloat16 [32, 1024, 1280], P('tm', 'tok')
The draws below stay inside these ranges and needn't reach their ends.
All inputs are finite; a program needn't handle non-finite values.
Results may differ from the reference program's by a relative error of at most 0.007.
The reference program's roundings to bfloat16 on the way count: a program that leaves them out, or rounds other values in their place, can miss the bound.
Values may be sent and summed in bfloat16 or wider, within the bound.
A program may use at most 64 MiB of HBM per device.

```python
import jax
import jax.numpy as jnp
from jax import lax

D = 1280
DH = 64
HEADS = 16
TOK_FRAME = 1024
FRAMES = 32


def draw_q_weight(key, part):
    key = jax.random.fold_in(key, 11)
    fresh = jax.random.normal(key, (D, HEADS * DH), jnp.float32)
    result = fresh * (8.0 / D) ** 0.5
    return jnp.clip(result, -0.5, 0.5).astype(jnp.bfloat16)


def draw_k_weight(key, part):
    key = jax.random.fold_in(key, 12)
    fresh = jax.random.normal(key, (D, HEADS * DH), jnp.float32)
    result = fresh * D ** (-0.5)
    return jnp.clip(result, -0.25, 0.25).astype(jnp.bfloat16)


def draw_hidden_states(key, part):
    key = jax.random.fold_in(key, 13)
    noise_key = jax.random.fold_in(key, 0)
    noise = jax.random.normal(noise_key, (FRAMES, TOK_FRAME, D), jnp.float32)
    result = noise
    return jnp.clip(result, -6.0, 6.0).astype(jnp.bfloat16)


def shard_levels(own_key, extent, cuts, smallest, top_value):
    level, own = 1.0, jax.random.fold_in(own_key, 6)
    for dim, shards_of in cuts:
        steps = jnp.exp(jax.random.uniform(jax.random.fold_in(own, dim), (shards_of,), jnp.float32, smallest / len(cuts), top_value / len(cuts)))
        level = level * jnp.repeat(steps, extent[dim] // shards_of).reshape([-1 if axis == dim else 1 for axis in range(len(extent))])
    return level


def scatter_about(key, shape, deviation, reach, cuts=(), held_as=jnp.bfloat16):
    values = deviation * jax.random.normal(key, shape, jnp.float32)
    if cuts:
        values = values * shard_levels(key, shape, cuts, -0.22, 0.18)
    return jnp.clip(values, -reach, reach).astype(held_as)


def setup_inputs(seed: int = 0) -> dict:
    seeds = jax.random.split(jax.random.key(seed), 8)
    hidden_states = draw_hidden_states(jax.random.fold_in(seeds[7], 71), 0)
    norm_gain = jnp.clip(1.0 + 0.18 * jax.random.normal(seeds[1], (D,), jnp.float32), 0.1, 1.9)
    norm_bias = scatter_about(seeds[2], (D,), 0.5, 3.0, (), jnp.float32)
    q_weight = draw_q_weight(jax.random.fold_in(seeds[7], 71), 0)
    k_weight = draw_k_weight(jax.random.fold_in(seeds[7], 71), 0)
    v_weight = scatter_about(seeds[5], (D, HEADS * DH), D ** -0.5, 0.15625, ((1, 16),))
    out_weight = scatter_about(seeds[6], (HEADS * DH, D), (HEADS * DH // 16) ** -0.5, 0.75, ((0, 16),))
    return {"hidden_states": hidden_states, "norm_gain": norm_gain, "norm_bias": norm_bias, "q_weight": q_weight, "k_weight": k_weight, "v_weight": v_weight, "out_weight": out_weight}


def layer_norm(states, norm_gain, norm_bias):
    widened = states.astype(jnp.float32)
    center = lax.optimization_barrier(jnp.mean(widened, axis=-1, keepdims=True))
    spread = lax.optimization_barrier(jnp.mean(jnp.square(widened - center), axis=-1, keepdims=True))
    scaled = (widened - center) * lax.rsqrt(spread + 1e-05)
    return (scaled * norm_gain.astype(jnp.float32) + norm_bias.astype(jnp.float32)).astype(jnp.bfloat16)

def attend_frame(queries, anchor_keys, anchor_values, earlier_keys, earlier_values):
    scale = DH ** (-0.5)
    query_wide = queries.astype(jnp.float32)
    scores_anchor = jnp.einsum('qhd,khd->hqk', query_wide, anchor_keys.astype(jnp.float32)) * scale
    scores_prev = jnp.einsum('qhd,khd->hqk', query_wide, earlier_keys.astype(jnp.float32)) * scale
    highest = jnp.maximum(lax.optimization_barrier(jnp.max(scores_anchor, axis=-1, keepdims=True)), lax.optimization_barrier(jnp.max(scores_prev, axis=-1, keepdims=True)))
    weights_anchor = jnp.exp(scores_anchor - highest)
    weights_prev = jnp.exp(scores_prev - highest)
    denominator = lax.optimization_barrier(jnp.sum(weights_anchor, axis=-1, keepdims=True)) + lax.optimization_barrier(jnp.sum(weights_prev, axis=-1, keepdims=True))
    probs_anchor = (weights_anchor / denominator).astype(jnp.bfloat16)
    probs_prev = (weights_prev / denominator).astype(jnp.bfloat16)
    mixed = jnp.einsum('hqk,khd->qhd', probs_anchor.astype(jnp.float32), anchor_values.astype(jnp.float32))
    mixed = mixed + jnp.einsum('hqk,khd->qhd', probs_prev.astype(jnp.float32), earlier_values.astype(jnp.float32))
    return mixed.astype(jnp.bfloat16)

def reference(hidden_states, norm_gain, norm_bias, q_weight, k_weight, v_weight, out_weight):
    normed = layer_norm(hidden_states, norm_gain, norm_bias)
    flattened = normed.reshape(FRAMES * TOK_FRAME, D)

    def project(weight):
        result = jnp.dot(flattened, weight, preferred_element_type=jnp.float32).astype(jnp.bfloat16)
        return result.reshape(FRAMES, TOK_FRAME, HEADS, DH)
    queries = project(q_weight)
    keys = project(k_weight)
    values = project(v_weight)

    def one_frame(position):
        earlier = jnp.maximum(position - 1, 0).astype(jnp.int32)
        query_frame = lax.dynamic_index_in_dim(queries, position, 0, keepdims=False)
        earlier_keys = lax.dynamic_index_in_dim(keys, earlier, 0, keepdims=False)
        earlier_values = lax.dynamic_index_in_dim(values, earlier, 0, keepdims=False)
        return attend_frame(query_frame, keys[0], values[0], earlier_keys, earlier_values)
    mixed = lax.map(one_frame, jnp.arange(FRAMES, dtype=jnp.int32))
    mixed = mixed.reshape(FRAMES * TOK_FRAME, HEADS * DH)
    result = jnp.dot(mixed, out_weight, preferred_element_type=jnp.float32).astype(jnp.bfloat16)
    return result.reshape(FRAMES, TOK_FRAME, D)
```

```python
import functools
import math

import jax
import jax.numpy as jnp
from jax import lax
from jax.experimental import pallas as pl
from jax.experimental.pallas import tpu as pltpu
from jax.sharding import PartitionSpec as P

MESH = pl.DeviceIdType.MESH
D = 1280
DH = 64
ROWS = 64
HALF = 32
TM = 32
TOK = 16
F32 = jnp.float32
BF16 = jnp.bfloat16
EXP_SCALE = DH ** (-0.5) / math.log(2.0)


def layer_norm(states, gain, bias):
    widened = states.astype(F32)
    center = jnp.mean(widened, axis=-1, keepdims=True)
    moved = widened - center
    spread = jnp.mean(jnp.square(moved), axis=-1, keepdims=True)
    return moved * lax.rsqrt(spread + 1e-05) * gain + bias


def kernel(
    x_hbm, gain_hbm, bias_hbm, wq_hbm, wk_hbm, wv_hbm, wo_hbm, o_ref,
    x_in, gain, bias, wq, wk, wv,
    wall, xg, wg, xf, apf, ap, apg, apgf, x0, akv, kv, pkv, qb, msend, mg, lhs,
    in_sem, tok_recv, tok_send, w_recv, w_send,
    sc_send, sc_recv, ap_send, ap_recv, an_send, an_recv,
    kv_send, kv_recv, mix_send, mix_recv, loc_sem,
):
    tm = lax.axis_index("tm")
    me = lax.axis_index("tok")
    y, x, c = me // 8, (me // 2) % 4, me % 2
    xp, xm, xa = (x + 1) % 4, (x + 3) % 4, (x + 2) % 4
    yo, co = 1 - y, 1 - c

    def tid(yy, xx, cc):
        return yy * 8 + xx * 2 + cc

    loads = []
    for i, (src, dst) in enumerate((
        (x_hbm.at[0], x_in), (gain_hbm, gain), (bias_hbm, bias), (wq_hbm, wq), (wk_hbm, wk), (wv_hbm, wv),
        (wo_hbm, wg.at[me]),
    )):
        load = pltpu.make_async_copy(src, dst, in_sem.at[i])
        load.start()
        loads.append(load)

    barrier = pltpu.get_barrier_semaphore()

    def greet_tok(i, carry):
        pl.semaphore_signal(barrier, inc=1, device_id=(tm, (me + i) % TOK), device_id_type=MESH)
        return carry

    def greet_tm(i, carry):
        pl.semaphore_signal(barrier, inc=1, device_id=((tm + i) % TM, me), device_id_type=MESH)
        return carry

    lax.fori_loop(1, TOK, greet_tok, 0)
    lax.fori_loop(1, TM, greet_tm, 0)

    for load in loads[:3]:
        load.wait()
    normed = layer_norm(x_in[...], gain[...], bias[...])
    xg[me] = normed.astype(BF16)

    @pl.when(tm == 0)
    def _():
        apf[...] = jnp.zeros_like(apf)
        xf[...] = normed
        for k in range(20):
            apf[pl.ds(k, TM, stride=32), :] = xf[(k % 2) * 32 : (k % 2) * 32 + 32, (k // 2) * 128 : (k // 2) * 128 + 128]
        ap[...] = apf[...].reshape(TM, 32, 128).astype(BF16)

    for load in loads[3:]:
        load.wait()
    wall[:, 0:128] = jnp.concatenate([wk[...], wv[...]], axis=1)
    wall[:, 128:256] = jnp.concatenate([wq[...], jnp.zeros_like(wq)], axis=1)

    pl.semaphore_wait(barrier, TOK - 1 + TM - 1)

    def scatter(j):
        return pltpu.make_async_remote_copy(
            src_ref=ap.at[j], dst_ref=apg.at[me], send_sem=sc_send.at[j], recv_sem=sc_recv,
            device_id=(j, me), device_id_type=MESH)

    @pl.when(tm == 0)
    def _():
        def go(j, carry):
            scatter(j).start()
            return carry
        lax.fori_loop(1, TM, go, 0)

    pending = []

    class Gather:
        def __init__(self, buf, send, recv):
            self.buf, self.send_sem, self.recv, self.count = buf, send, recv, 0

        def part(self, block, half):
            return self.buf.at[block, pl.ds(half * HALF, HALF)]

        def send(self, block, half, to):
            copy = pltpu.make_async_remote_copy(
                src_ref=self.part(block, half), dst_ref=self.part(block, half),
                send_sem=self.send_sem.at[self.count], recv_sem=self.recv.at[block * 2 + half],
                device_id=(tm, to), device_id_type=MESH)
            self.count += 1
            copy.start()
            pending.append(copy)

        def wait(self, block, half):
            part = self.part(block, half)
            pltpu.make_async_copy(part, part, self.recv.at[block * 2 + half]).wait()

        def wait_block(self, block):
            self.wait(block, 0)
            self.wait(block, 1)

    right, left, over, twin = tid(y, xp, c), tid(y, xm, c), tid(yo, x, c), tid(y, x, co)
    tok = Gather(xg, tok_send, tok_recv)
    out = Gather(wg, w_send, w_recv)

    def own_y(g):
        g.send(me, 0, over)
        g.send(me, 1, over)

    def own_x(g):
        for half in (0, 1):
            g.send(me, half, right)
            g.send(me, half, left)
            g.send(me, half, twin)

    def relay(g, yy):
        from_left, from_right = tid(yy, xm, c), tid(yy, xp, c)
        g.wait(from_left, 0)
        g.send(from_left, 0, right)
        g.wait(from_right, 1)
        g.send(from_right, 1, left)
        g.send(from_left, 0, twin)
        g.send(from_right, 1, twin)
        g.wait(from_left, 1)
        g.send(from_left, 1, twin)
        g.wait(from_right, 0)
        g.send(from_right, 0, twin)

    def spread_over(g):
        for half in (0, 1):
            g.wait(over, half)
            g.send(over, half, right)
            g.send(over, half, left)
            g.send(over, half, twin)

    def far(g, yy):
        block = tid(yy, xa, c)
        for half in (0, 1):
            g.wait(block, half)
            g.send(block, half, twin)

    def kv_copy(chip):
        rows = pl.ds(chip * 128, 128)
        return pltpu.make_async_remote_copy(
            src_ref=kv.at[rows], dst_ref=pkv.at[rows], send_sem=kv_send.at[chip], recv_sem=kv_recv.at[chip],
            device_id=(jnp.minimum(tm + 1, TM - 1), me), device_id_type=MESH)

    def project(yy, xx):
        chip = yy * 4 + xx
        tokens = xg[pl.ds(chip * 2, 2)].reshape(128, D)
        made = jnp.dot(tokens, wall[...], preferred_element_type=F32).astype(BF16)
        rows = pl.ds(chip * 128, 128)
        kv[rows] = made[:, 0:128]
        qb[rows] = made[:, 128:256]

        @pl.when(tm < TM - 1)
        def _():
            kv_copy(chip).start()

    own_y(tok)
    own_x(tok)
    tok.wait_block(twin)
    project(y, x)
    relay(tok, y)

    @pl.when(tm > 0)
    def _():
        pltpu.make_async_copy(apg.at[me], apg.at[me], sc_recv).wait()

    @pl.when(tm == 0)
    def _():
        apg[me] = ap[0]

    def piece(i):
        to = (me + i) % TOK
        return pltpu.make_async_remote_copy(
            src_ref=apg.at[me], dst_ref=apg.at[me], send_sem=ap_send.at[i], recv_sem=ap_recv.at[me],
            device_id=(tm, to), device_id_type=MESH)

    def send_piece(i, carry):
        piece(i).start()
        return carry

    lax.fori_loop(1, TOK, send_piece, 0)

    for xx in (xm, xp):
        tok.wait_block(tid(y, xx, co))
        project(y, xx)
    spread_over(tok)
    far(tok, y)

    def wait_piece(i, carry):
        s = (me + i) % TOK
        pltpu.make_async_copy(apg.at[s], apg.at[s], ap_recv.at[s]).wait()
        return carry

    lax.fori_loop(1, TOK, wait_piece, 0)
    apgf[...] = apg[...].astype(F32).reshape(TOK * 32, 128)
    for k in range(20):
        x0[(k % 2) * 16 : (k % 2) * 16 + 16, (k // 2) * 128 : (k // 2) * 128 + 128] = (
            apgf[pl.ds(k, TOK, stride=32), :].astype(BF16))
    akv[pl.ds(tm * 32, 32)] = jnp.dot(x0[...], wall[:, 0:128], preferred_element_type=F32).astype(BF16)

    def anchor(i):
        rows = pl.ds(tm * 32, 32)
        return pltpu.make_async_remote_copy(
            src_ref=akv.at[rows], dst_ref=akv.at[rows], send_sem=an_send.at[i], recv_sem=an_recv.at[tm],
            device_id=((tm + i) % TM, me), device_id_type=MESH)

    def send_anchor(i, carry):
        anchor(i).start()
        return carry

    lax.fori_loop(1, TM, send_anchor, 0)

    tok.wait_block(tid(y, xa, co))
    project(y, xa)
    own_y(out)
    tok.wait_block(tid(yo, x, co))
    project(yo, x)
    relay(tok, yo)
    for xx in (xm, xp):
        tok.wait_block(tid(yo, xx, co))
        project(yo, xx)
    far(tok, yo)
    own_x(out)
    tok.wait_block(tid(yo, xa, co))
    project(yo, xa)

    def wait_anchor(i, carry):
        rows = pl.ds(((tm + i) % TM) * 32, 32)
        pltpu.make_async_copy(akv.at[rows], akv.at[rows], an_recv.at[(tm + i) % TM]).wait()
        return carry

    lax.fori_loop(1, TM, wait_anchor, 0)

    @pl.when(tm == 0)
    def _():
        copy = pltpu.make_async_copy(kv, pkv, loc_sem)
        copy.start()
        copy.wait()

    @pl.when(tm > 0)
    def _():
        for chip in range(8):
            rows = pl.ds(chip * 128, 128)
            pltpu.make_async_copy(pkv.at[rows], pkv.at[rows], kv_recv.at[chip]).wait()

    low = lax.broadcasted_iota(jnp.int32, (HALF, 128), 1) < DH
    nt = (((1,), (1,)), ((), ()))

    def mix_copy(to):
        return pltpu.make_async_remote_copy(
            src_ref=msend.at[to], dst_ref=mg.at[me], send_sem=mix_send.at[to], recv_sem=mix_recv.at[me],
            device_id=(tm, to), device_id_type=MESH)

    def attend(i):
        yy = (y + 1 + i // 2) % 2
        pp = (x // 2 + 1 + i) % 2
        first = yy * 8 + pp * 4
        queries = qb[pl.ds(first * ROWS, 4 * ROWS)]
        s_a = lax.dot_general(queries, akv[...], nt, preferred_element_type=F32)
        s_p = lax.dot_general(queries, pkv[...], nt, preferred_element_type=F32)
        highest = jnp.maximum(jnp.max(s_a, axis=-1, keepdims=True), jnp.max(s_p, axis=-1, keepdims=True))
        e_a = jnp.exp2((s_a - highest) * EXP_SCALE)
        e_p = jnp.exp2((s_p - highest) * EXP_SCALE)
        inverse = 1.0 / (jnp.sum(e_a, axis=-1, keepdims=True) + jnp.sum(e_p, axis=-1, keepdims=True))
        p_a = (e_a * inverse).astype(BF16)
        p_p = (e_p * inverse).astype(BF16)
        mixed = jnp.dot(p_a, akv[...], preferred_element_type=F32) + jnp.dot(p_p, pkv[...], preferred_element_type=F32)
        for k in range(4):
            top = mixed[k * ROWS : k * ROWS + HALF]
            bottom = mixed[k * ROWS + HALF : (k + 1) * ROWS]
            msend[first + k] = jnp.where(low, pltpu.roll(top, DH, 1), bottom).astype(BF16)
            to = first + k

            @pl.when(to != me)
            def _():
                mix_copy(to).start()

    def two(start):
        lax.fori_loop(start, start + 2, lambda i, carry: (attend(i), carry)[1], 0)

    two(0)
    relay(out, y)
    spread_over(out)
    two(2)
    far(out, y)
    relay(out, yo)
    far(out, yo)
    mg[me] = msend[me]

    def wait_mix(i, carry):
        s = (me + i) % TOK
        pltpu.make_async_copy(mg.at[s], mg.at[s], mix_recv.at[s]).wait()
        return carry

    lax.fori_loop(1, TOK, wait_mix, 0)
    for i in range(8):
        even = mg[2 * i].astype(F32)
        odd = mg[2 * i + 1].astype(F32)
        lhs[0:HALF, i * 128 : (i + 1) * 128] = jnp.where(low, even, pltpu.roll(odd, DH, 1)).astype(BF16)
        lhs[HALF:ROWS, i * 128 : (i + 1) * 128] = jnp.where(low, pltpu.roll(even, DH, 1), odd).astype(BF16)
    for yy in (0, 1):
        for xx in range(4):
            @pl.when((yy != y) | (xx != x))
            def _():
                out.wait_block(tid(yy, xx, co))
    out.wait_block(twin)
    o_ref[0] = jnp.dot(lhs[...], wg[...].reshape(TOK * DH, D), preferred_element_type=F32).astype(BF16)

    for copy in pending:
        copy.wait_send()

    def drain_tok(i, carry):
        piece(i).wait_send()
        mix_copy((me + i) % TOK).wait_send()
        return carry

    def drain_tm(i, carry):
        anchor(i).wait_send()
        return carry

    lax.fori_loop(1, TOK, drain_tok, 0)
    lax.fori_loop(1, TM, drain_tm, 0)

    @pl.when(tm == 0)
    def _():
        def drain(j, carry):
            scatter(j).wait_send()
            return carry
        lax.fori_loop(1, TM, drain, 0)

    @pl.when(tm < TM - 1)
    def _():
        for chip in range(8):
            kv_copy(chip).wait_send()


def body(hidden_states, norm_gain, norm_bias, q_weight, k_weight, v_weight, out_weight):
    anywhere = pl.BlockSpec(memory_space=pl.ANY)
    vmem = pltpu.VMEM
    dma = pltpu.SemaphoreType.DMA
    return pl.pallas_call(
        kernel,
        out_shape=jax.ShapeDtypeStruct((1, ROWS, D), BF16),
        in_specs=[anywhere] * 7,
        out_specs=pl.BlockSpec(memory_space=pltpu.VMEM),
        scratch_shapes=[
            vmem((ROWS, D), BF16), vmem((1, D), F32), vmem((1, D), F32),
            vmem((D, DH), BF16), vmem((D, DH), BF16), vmem((D, DH), BF16),
            vmem((D, 256), BF16),
            vmem((TOK, ROWS, D), BF16),
            vmem((TOK, ROWS, D), BF16),
            vmem((ROWS, D), F32),
            vmem((TM * 32, 128), F32),
            vmem((TM, 32, 128), BF16),
            vmem((TOK, 32, 128), BF16),
            vmem((TOK * 32, 128), F32),
            vmem((32, D), BF16),
            vmem((1024, 128), BF16),
            vmem((1024, 128), BF16),
            vmem((1024, 128), BF16),
            vmem((1024, 128), BF16),
            vmem((TOK, HALF, 128), BF16),
            vmem((TOK, HALF, 128), BF16),
            vmem((ROWS, TOK * DH), BF16),
            dma((7,)), dma((32,)), dma((40,)), dma((32,)), dma((40,)),
            dma((TM,)), dma, dma((TOK,)), dma((TOK,)), dma((TM,)), dma((TM,)),
            dma((8,)), dma((8,)), dma((TOK,)), dma((TOK,)), dma,
        ],
        compiler_params=pltpu.CompilerParams(
            collective_id=0, has_side_effects=True, vmem_limit_bytes=40 * 2**20),
        cost_estimate=pl.CostEstimate(flops=1_200_000_000, bytes_accessed=2_000_000, transcendentals=2_000_000),
        name="cross_frame_attention",
    )(hidden_states, norm_gain.reshape(1, D), norm_bias.reshape(1, D), q_weight, k_weight, v_weight, out_weight)


def solution(mesh):
    return jax.shard_map(
        body,
        mesh=mesh,
        in_specs=(P("tm", "tok", None), P(), P(), P(None, "tok"), P(None, "tok"), P(None, "tok"), P("tok", None)),
        out_specs=P("tm", "tok", None),
        check_vma=False,
    )
```

```python
import functools
import math

import jax
import jax.numpy as jnp
from jax import lax
from jax.experimental import pallas as pl
from jax.experimental.pallas import tpu as pltpu
from jax.sharding import PartitionSpec as P

MESH = pl.DeviceIdType.MESH
D = 1280
DH = 64
ROWS = 64
HALF = 32
TM = 32
TOK = 16
F32 = jnp.float32
BF16 = jnp.bfloat16
EXP_SCALE = DH ** (-0.5) / math.log(2.0)


def layer_norm(states, gain, bias):
    widened = states.astype(F32)
    center = jnp.mean(widened, axis=-1, keepdims=True)
    moved = widened - center
    spread = jnp.mean(jnp.square(moved), axis=-1, keepdims=True)
    return moved * lax.rsqrt(spread + 1e-05) * gain + bias


def kernel(
    x_hbm, gain_hbm, bias_hbm, wq_hbm, wk_hbm, wv_hbm, wo_hbm, o_ref,
    x_in, gain, bias, wall_t,
    wall, xg, wg, xf, apf, ap, apz, apg, apgf, x0, akv, kv, pkv, qb, e_prev, m_prev, l_prev, msend, mg, lhs,
    in_sem, tok_recv, tok_send, w_recv, w_send,
    sc_send, sc_recv, sy_send, sy_recv, ap_send, ap_recv, an_send, an_recv,
    kv_send, kv_recv, mix_send, mix_recv, loc_sem,
):
    tm = lax.axis_index("tm")
    y_lo, z = tm // 8, tm % 8
    me = lax.axis_index("tok")
    y, x, c = me // 8, (me // 2) % 4, me % 2
    xp, xm, xa = (x + 1) % 4, (x + 3) % 4, (x + 2) % 4
    yo, co = 1 - y, 1 - c

    def tid(yy, xx, cc):
        return yy * 8 + xx * 2 + cc

    loads = []
    for i, (src, dst) in enumerate((
        (x_hbm.at[0], x_in), (gain_hbm, gain), (bias_hbm, bias),
        (wk_hbm, wall_t.at[pl.ds(0, DH)]), (wv_hbm, wall_t.at[pl.ds(DH, DH)]), (wq_hbm, wall_t.at[pl.ds(2 * DH, DH)]),
        (wo_hbm, wg.at[me]),
    )):
        load = pltpu.make_async_copy(src, dst, in_sem.at[i])
        load.start()
        loads.append(load)

    barrier = pltpu.get_barrier_semaphore()

    def greet_tok(i, carry):
        pl.semaphore_signal(barrier, inc=1, device_id=(tm, (me + i) % TOK), device_id_type=MESH)
        return carry

    def greet_z(i, carry):
        pl.semaphore_signal(barrier, inc=1, device_id=(y_lo * 8 + (z + i) % 8, me), device_id_type=MESH)
        return carry

    def greet_y(i, carry):
        pl.semaphore_signal(barrier, inc=1, device_id=((tm + 8 * i) % TM, me), device_id_type=MESH)
        return carry

    lax.fori_loop(1, 4, greet_y, 0)
    lax.fori_loop(1, 8, greet_z, 0)
    for step in (1, TM - 1):
        pl.semaphore_signal(barrier, inc=1, device_id=((tm + step) % TM, me), device_id_type=MESH)
    lax.fori_loop(1, TOK, greet_tok, 0)

    for load in loads[:3]:
        load.wait()
    normed = layer_norm(x_in[...], gain[...].reshape(1, D), bias[...].reshape(1, D))
    xg[me] = normed.astype(BF16)

    @pl.when(tm == 0)
    def _():
        apf[...] = jnp.zeros_like(apf)
        xf[...] = normed
        for k in range(20):
            apf[pl.ds(k, TM, stride=32), :] = xf[(k % 2) * 32 : (k % 2) * 32 + 32, (k // 2) * 128 : (k // 2) * 128 + 128]
        ap[...] = apf[...].reshape(8, 4, 32, 128).astype(BF16)

    wall_t[3 * DH :] = jnp.zeros((DH, D), BF16)
    for load in loads[3:]:
        load.wait()
    wall[...] = wall_t[...].T

    pl.semaphore_wait(barrier, TOK - 1 + 7 + 3 + 2)

    def scatter(j):
        return pltpu.make_async_remote_copy(
            src_ref=ap.at[j], dst_ref=apz, send_sem=sc_send.at[j], recv_sem=sc_recv,
            device_id=(j, me), device_id_type=MESH)

    def scatter_y(k):
        return pltpu.make_async_remote_copy(
            src_ref=apz.at[k], dst_ref=apg.at[me], send_sem=sy_send.at[k], recv_sem=sy_recv,
            device_id=(k * 8 + z, me), device_id_type=MESH)

    @pl.when(tm == 0)
    def _():
        for j in (4, 3, 5, 2, 6, 1, 7):
            scatter(j).start()
        apz[...] = ap[0]

    class Gather:
        def __init__(self, buf, send, recv):
            self.buf, self.send_sem, self.recv, self.count, self.sent = buf, send, recv, 0, []

        def part(self, block, piece):
            return self.buf.at[block, pl.ds(piece[0], piece[1])]

        def send(self, block, piece, to, group=None):
            copy = pltpu.make_async_remote_copy(
                src_ref=self.part(block, piece), dst_ref=self.part(block, piece),
                send_sem=self.send_sem.at[self.count], recv_sem=self.recv.at[block * 4 + piece[0] // 16],
                device_id=(tm if group is None else group, to), device_id_type=MESH)
            self.count += 1
            copy.start()
            self.sent.append(copy)

        def wait(self, block, piece):
            part = self.part(block, piece)
            pltpu.make_async_copy(part, part, self.recv.at[block * 4 + piece[0] // 16]).wait()

        def wait_block(self, block, pieces):
            for piece in pieces:
                self.wait(block, piece)

    halves = ((0, 32), (32, 32))
    quarters = ((0, 16), (16, 16), (32, 16), (48, 16))
    right, left, over, twin = tid(y, xp, c), tid(y, xm, c), tid(yo, x, c), tid(y, x, co)
    tok = Gather(xg, tok_send, tok_recv)
    out = Gather(wg, w_send, w_recv)

    def own_x(g):
        for piece in halves:
            g.send(me, piece, right)
            g.send(me, piece, left)
        for piece in halves:
            g.send(me, piece, twin)

    def relay_even(g, yy, even):
        from_left, from_right = tid(yy, xm, c), tid(yy, xp, c)
        g.wait(from_left, even)
        g.send(from_left, even, right)
        g.wait(from_right, even)
        g.send(from_left, even, twin)
        g.send(from_right, even, twin)

    def relay_odd(g, yy, odd):
        from_left, from_right = tid(yy, xm, c), tid(yy, xp, c)
        g.wait(from_right, odd)
        g.send(from_right, odd, left)
        g.wait(from_left, odd)
        g.send(from_left, odd, twin)
        g.send(from_right, odd, twin)

    def relay(g, yy, pieces):
        for even, odd in zip(pieces[::2], pieces[1::2]):
            relay_even(g, yy, even)
            relay_odd(g, yy, odd)

    def spread_over(g, piece):
        g.send(over, piece, right)
        g.send(over, piece, left)
        g.send(over, piece, twin)

    def far(g, yy, pieces):
        block = tid(yy, xa, c)
        for piece in pieces:
            g.wait(block, piece)
            g.send(block, piece, twin)

    def kv_copy(chip):
        rows = pl.ds(chip * 128, 128)
        return pltpu.make_async_remote_copy(
            src_ref=kv.at[rows], dst_ref=pkv.at[rows], send_sem=kv_send.at[chip], recv_sem=kv_recv.at[chip],
            device_id=(jnp.minimum(tm + 1, TM - 1), me), device_id_type=MESH)

    def project(yy, xx):
        chip = yy * 4 + xx
        tokens = xg[pl.ds(chip * 2, 2)].reshape(128, D)
        made = jnp.dot(tokens, wall[...], preferred_element_type=F32).astype(BF16)
        rows = pl.ds(chip * 128, 128)
        kv[rows] = made[:, 0:128]
        qb[rows] = made[:, 128:256]

        @pl.when(tm < TM - 1)
        def _():
            kv_copy(chip).start()

    def rows_copy(i):
        return pltpu.make_async_remote_copy(
            src_ref=apg.at[me], dst_ref=apg.at[me], send_sem=ap_send.at[i], recv_sem=ap_recv.at[me],
            device_id=(tm, (me + i) % TOK), device_id_type=MESH)

    def wait_rows(slot):
        pltpu.make_async_copy(apg.at[slot], apg.at[slot], ap_recv.at[slot]).wait()

    def each(start, stop, step):
        lax.fori_loop(start, stop, lambda i, carry: (step(i), carry)[1], 0)

    def half_z(zz):
        return pl.ds(y_lo * 128 + zz * 16, 16)

    def half_zy(yy):
        return pl.ds(yy * 128, 128)

    def half_y(yy):
        return pl.ds(512 + z * 64 + yy * 16, 16)

    def half_yz(zz):
        return pl.ds(512 + zz * 64, 64)

    def anchor(rows, n, source, to):
        return pltpu.make_async_remote_copy(
            src_ref=akv.at[rows], dst_ref=akv.at[rows], send_sem=an_send.at[n], recv_sem=an_recv.at[source],
            device_id=(to, me), device_id_type=MESH)

    def wait_anchor(rows, source):
        pltpu.make_async_copy(akv.at[rows], akv.at[rows], an_recv.at[source]).wait()

    def anchor_z(i):
        return anchor(half_z(z), i, z, y_lo * 8 + (z + i) % 8)

    def anchor_y(i):
        return anchor(half_y(y_lo), 8 + i, 8 + y_lo, (tm + 8 * i) % TM)

    def anchor_zy(i):
        return anchor(half_zy(y_lo), 12 + i, 12 + y_lo, (tm + 8 * i) % TM)

    def anchor_yz(i):
        return anchor(half_yz(z), 16 + i, 16 + z, y_lo * 8 + (z + i) % 8)

    def over_in(piece):
        tok.wait(over, piece)
        spread_over(tok, piece)

    tok.send(me, quarters[0], over)
    tok.send(me, halves[0], right)
    tok.send(me, halves[0], left)
    tok.send(me, quarters[1], over)
    tok.send(me, halves[1], right)
    tok.send(me, halves[1], left)
    tok.send(me, quarters[2], over)
    tok.send(me, halves[0], twin)
    tok.send(me, halves[1], twin)
    tok.send(me, quarters[3], over)

    tok.wait_block(twin, halves)
    project(y, x)

    @pl.when(tm < 8)
    def _():
        @pl.when(tm > 0)
        def _():
            pltpu.make_async_copy(apz, apz, sc_recv).wait()
        for k in (3, 2, 1):
            scatter_y(k).start()
        apg[me] = apz[0]

    relay_even(tok, y, halves[0])
    over_in(quarters[0])
    relay_odd(tok, y, halves[1])
    over_in(quarters[1])

    for xx in (xm, xp):
        tok.wait_block(tid(y, xx, co), halves)
        project(y, xx)
    over_in(quarters[2])
    over_in(quarters[3])

    @pl.when(tm >= 8)
    def _():
        pltpu.make_async_copy(apg.at[me], apg.at[me], sy_recv).wait()

    each(1, TOK, lambda i: rows_copy(i).start())
    far(tok, y, halves)
    relay(tok, yo, quarters[:2])
    tok.wait_block(tid(y, xa, co), halves)
    project(y, xa)
    relay(tok, yo, quarters[2:])
    mine, theirs = (32 * (z % 2), 32), (32 - 32 * (z % 2), 32)
    out.send(me, mine, over)
    own_x(out)
    tok.wait_block(tid(yo, x, co), quarters)
    project(yo, x)
    for xx in (xm, xp):
        tok.wait_block(tid(yo, xx, co), quarters)
        project(yo, xx)

    each(1, TOK, lambda i: wait_rows((me + i) % TOK))
    apgf[...] = apg[...].astype(F32).reshape(TOK * 32, 128)
    for k in range(20):
        x0[(k % 2) * 16 : (k % 2) * 16 + 16, (k // 2) * 128 : (k // 2) * 128 + 128] = (
            apgf[pl.ds(k, TOK, stride=32), :].astype(BF16))
    made = jnp.dot(x0[...], wall[:, 0:128], preferred_element_type=F32).astype(BF16)
    akv[half_z(z)] = made[0:16]
    akv[half_y(y_lo)] = made[16:32]
    each(1, 4, lambda i: anchor_y(i).start())
    each(1, 8, lambda i: anchor_z(i).start())

    far(tok, yo, quarters)
    tok.wait_block(tid(yo, xa, co), quarters)
    project(yo, xa)
    out.wait(over, mine)
    out.send(over, mine, me, tm + 1 - 2 * (z % 2))
    each(1, 4, lambda i: wait_anchor(half_y((y_lo + i) % 4), 8 + (y_lo + i) % 4))
    each(1, 8, lambda i: anchor_yz(i).start())
    each(1, 8, lambda i: wait_anchor(half_z((z + i) % 8), (z + i) % 8))
    each(1, 4, lambda i: anchor_zy(i).start())

    @pl.when(tm == 0)
    def _():
        copy = pltpu.make_async_copy(kv, pkv, loc_sem)
        copy.start()
        copy.wait()

    @pl.when(tm > 0)
    def _():
        for chip in range(8):
            rows = pl.ds(chip * 128, 128)
            pltpu.make_async_copy(pkv.at[rows], pkv.at[rows], kv_recv.at[chip]).wait()

    low = lax.broadcasted_iota(jnp.int32, (HALF, 128), 1) < DH
    nt = (((1,), (1,)), ((), ()))

    def mix_copy(to):
        return pltpu.make_async_remote_copy(
            src_ref=msend.at[to], dst_ref=mg.at[me], send_sem=mix_send.at[to], recv_sem=mix_recv.at[me],
            device_id=(tm, to), device_id_type=MESH)

    def chunk(i):
        yy = (y + 1 + i // 2) % 2
        pp = (x // 2 + 1 + i) % 2
        return yy * 8 + pp * 4

    def attend_prev(i):
        rows = pl.ds(chunk(i) * ROWS, 4 * ROWS)
        scores = lax.dot_general(qb[rows], pkv[...], nt, preferred_element_type=F32)
        highest = jnp.max(scores, axis=-1, keepdims=True)
        weights = jnp.exp2((scores - highest) * EXP_SCALE)
        e_prev[rows] = weights
        m_prev[rows] = jnp.broadcast_to(highest, (4 * ROWS, 128))
        l_prev[rows] = jnp.broadcast_to(jnp.sum(weights, axis=-1, keepdims=True), (4 * ROWS, 128))

    def attend(i):
        first = chunk(i)
        rows = pl.ds(first * ROWS, 4 * ROWS)
        scores = lax.dot_general(qb[rows], akv[...], nt, preferred_element_type=F32)
        before = m_prev[rows][:, 0:1]
        highest = jnp.maximum(jnp.max(scores, axis=-1, keepdims=True), before)
        weights = jnp.exp2((scores - highest) * EXP_SCALE)
        shrink = jnp.exp2((before - highest) * EXP_SCALE)
        inverse = 1.0 / (jnp.sum(weights, axis=-1, keepdims=True) + l_prev[rows][:, 0:1] * shrink)
        p_a = (weights * inverse).astype(BF16)
        p_p = (e_prev[rows] * (shrink * inverse)).astype(BF16)
        mixed = jnp.dot(p_a, akv[...], preferred_element_type=F32) + jnp.dot(p_p, pkv[...], preferred_element_type=F32)
        for k in range(4):
            top = mixed[k * ROWS : k * ROWS + HALF]
            bottom = mixed[k * ROWS + HALF : (k + 1) * ROWS]
            msend[first + k] = jnp.where(low, pltpu.roll(top, DH, 1), bottom).astype(BF16)
            to = first + k

            @pl.when(to != me)
            def _():
                mix_copy(to).start()

    out.wait(over, theirs)
    for piece in halves:
        spread_over(out, piece)
    each(0, 4, attend_prev)
    relay(out, y, halves)
    each(1, 8, lambda i: wait_anchor(half_yz((z + i) % 8), 16 + (z + i) % 8))
    each(1, 4, lambda i: wait_anchor(half_zy((y_lo + i) % 4), 12 + (y_lo + i) % 4))
    each(0, 2, attend)
    relay(out, yo, halves)
    far(out, y, halves)
    each(2, 4, attend)
    far(out, yo, halves)
    mg[me] = msend[me]

    def drain_mix(i, carry):
        mix_copy((me + i) % TOK).wait_send()
        return carry

    each(1, TOK, lambda i: rows_copy(i).wait_send())
    each(1, 8, lambda i: anchor_z(i).wait_send())
    each(1, 4, lambda i: anchor_y(i).wait_send())
    each(1, 4, lambda i: anchor_zy(i).wait_send())
    each(1, 8, lambda i: anchor_yz(i).wait_send())

    @pl.when(tm == 0)
    def _():
        for j in range(1, 8):
            scatter(j).wait_send()

    @pl.when(tm < 8)
    def _():
        for k in range(1, 4):
            scatter_y(k).wait_send()

    @pl.when(tm < TM - 1)
    def _():
        for chip in range(8):
            kv_copy(chip).wait_send()

    for copy in tok.sent:
        copy.wait_send()

    def wait_mix(i, carry):
        s = (me + i) % TOK
        pltpu.make_async_copy(mg.at[s], mg.at[s], mix_recv.at[s]).wait()
        return carry

    lax.fori_loop(1, TOK, wait_mix, 0)
    for i in range(8):
        even = mg[2 * i].astype(F32)
        odd = mg[2 * i + 1].astype(F32)
        lhs[0:HALF, i * 128 : (i + 1) * 128] = jnp.where(low, even, pltpu.roll(odd, DH, 1)).astype(BF16)
        lhs[HALF:ROWS, i * 128 : (i + 1) * 128] = jnp.where(low, pltpu.roll(even, DH, 1), odd).astype(BF16)
    for yy in (0, 1):
        for xx in range(4):
            @pl.when((yy != y) | (xx != x))
            def _():
                out.wait_block(tid(yy, xx, co), halves)
    out.wait_block(twin, halves)
    o_ref[0] = jnp.dot(lhs[...], wg[...].reshape(TOK * DH, D), preferred_element_type=F32).astype(BF16)

    for copy in out.sent:
        copy.wait_send()
    lax.fori_loop(1, TOK, drain_mix, 0)


def body(hidden_states, norm_gain, norm_bias, q_weight, k_weight, v_weight, out_weight):
    anywhere = pl.BlockSpec(memory_space=pltpu.HBM)
    vmem = pltpu.VMEM
    dma = pltpu.SemaphoreType.DMA
    return pl.pallas_call(
        kernel,
        out_shape=jax.ShapeDtypeStruct((1, ROWS, D), BF16),
        in_specs=[anywhere] * 7,
        out_specs=pl.BlockSpec(memory_space=pltpu.VMEM),
        scratch_shapes=[
            vmem((ROWS, D), BF16), vmem((D,), F32), vmem((D,), F32),
            vmem((256, D), BF16),
            vmem((D, 256), BF16),
            vmem((TOK, ROWS, D), BF16),
            vmem((TOK, ROWS, D), BF16),
            vmem((ROWS, D), F32),
            vmem((TM * 32, 128), F32),
            vmem((8, 4, 32, 128), BF16),
            vmem((4, 32, 128), BF16),
            vmem((TOK, 32, 128), BF16),
            vmem((TOK * 32, 128), F32),
            vmem((32, D), BF16),
            vmem((1024, 128), BF16),
            vmem((1024, 128), BF16),
            vmem((1024, 128), BF16),
            vmem((1024, 128), BF16),
            vmem((1024, 1024), F32),
            vmem((1024, 128), F32),
            vmem((1024, 128), F32),
            vmem((TOK, HALF, 128), BF16),
            vmem((TOK, HALF, 128), BF16),
            vmem((ROWS, TOK * DH), BF16),
            dma((7,)), dma((64,)), dma((64,)), dma((64,)), dma((64,)),
            dma((8,)), dma, dma((4,)), dma, dma((TOK,)), dma((TOK,)), dma((24,)), dma((24,)),
            dma((8,)), dma((8,)), dma((TOK,)), dma((TOK,)), dma,
        ],
        compiler_params=pltpu.CompilerParams(
            collective_id=0, has_side_effects=True, vmem_limit_bytes=63 * 2**20 + 2**19),
        cost_estimate=pl.CostEstimate(flops=1_200_000_000, bytes_accessed=2_000_000, transcendentals=2_000_000),
        name="cross_frame_attention",
    )(hidden_states, norm_gain, norm_bias, q_weight.T, k_weight.T, v_weight.T, out_weight)


def solution(mesh):
    return jax.shard_map(
        body,
        mesh=mesh,
        in_specs=(P("tm", "tok", None), P(), P(), P(None, "tok"), P(None, "tok"), P(None, "tok"), P("tok", None)),
        out_specs=P("tm", "tok", None),
        check_vma=False,
    )
```

```python
import functools
import math

import jax
import jax.numpy as jnp
from jax import lax
from jax.experimental import pallas as pl
from jax.experimental.pallas import tpu as pltpu
from jax.sharding import PartitionSpec as P

MESH = pl.DeviceIdType.MESH
D = 1280
DH = 64
ROWS = 64
HALF = 32
TM = 32
TOK = 16
F32 = jnp.float32
BF16 = jnp.bfloat16
VMEM_LIMIT = 63 * 2**20
EXP_SCALE = DH ** (-0.5) / math.log(2.0)


def layer_norm(states, gain, bias):
    widened = states.astype(F32)
    center = jnp.mean(widened, axis=-1, keepdims=True)
    moved = widened - center
    spread = jnp.mean(jnp.square(moved), axis=-1, keepdims=True)
    return moved * lax.rsqrt(spread + 1e-05) * gain + bias


def kernel(
    x_hbm, gain_hbm, bias_hbm, wq_hbm, wk_hbm, wv_hbm, wo_hbm, o_ref,
    x_in, gain, bias, wall_t,
    wall, xg, wg, kv, keyval, qb, e_first, m_first, l_first, msend, mg, lhs,
    in_sem, tok_send, tok_recv, out_send, out_recv,
    down_send, down_recv, anchor_send, anchor_recv, kv_send, kv_recv, mix_send, mix_recv,
    tok_ready, tm_ready,
):
    tm = lax.axis_index("tm")
    y_lo, z = tm // 8, tm % 8
    me = lax.axis_index("tok")
    y, x, c = me // 8, (me // 2) % 4, me % 2
    xp, xm, xa = (x + 1) % 4, (x + 3) % 4, (x + 2) % 4
    yo, co = 1 - y, 1 - c

    def tid(yy, xx, cc):
        return yy * 8 + xx * 2 + cc

    def each(start, stop, step):
        lax.fori_loop(start, stop, lambda i, carry: (step(i), carry)[1], 0)

    def wait(ref, sem):
        pltpu.make_async_copy(ref, ref, sem).wait()

    def remote(src, dst, send_sem, recv_sem, group, to):
        return pltpu.make_async_remote_copy(
            src_ref=src, dst_ref=dst, send_sem=send_sem, recv_sem=recv_sem,
            device_id=(group, to), device_id_type=MESH)

    for i, src, dst in (
        (0, x_hbm.at[0], x_in), (1, gain_hbm, gain), (2, bias_hbm, bias),
        (3, wk_hbm, wall_t.at[pl.ds(0, DH)]), (3, wv_hbm, wall_t.at[pl.ds(DH, DH)]),
        (3, wq_hbm, wall_t.at[pl.ds(2 * DH, DH)]), (4, wo_hbm, wg.at[me]),
    ):
        pltpu.make_async_copy(src, dst, in_sem.at[i]).start()

    barrier = pltpu.get_barrier_semaphore()

    def greet(group, to):
        pl.semaphore_signal(barrier, inc=1, device_id=(group, to), device_id_type=MESH)

    @pl.when(c == 0)
    def _():
        greet(tm, me + 1)

    @pl.when(c == 1)
    def _():
        greet(tm, me - 1)

    each(1, 8, lambda i: greet(tm, (me + 2 * i) % TOK - c))
    far_side = tid(y, x, 1)
    each(1, 4, lambda i: greet((tm + 8 * i) % TM, far_side))
    each(1, 8, lambda i: greet(y_lo * 8 + (z + i) % 8, far_side))
    greet((tm + 1) % TM, far_side)
    greet((tm + TM - 1) % TM, far_side)

    wait(x_in, in_sem.at[0])
    wait(gain, in_sem.at[1])
    wait(bias, in_sem.at[2])
    normed = layer_norm(x_in[...], gain[...].reshape(1, D), bias[...].reshape(1, D))
    xg[me] = normed.astype(BF16)

    wall_t[3 * DH :] = jnp.zeros((DH, D), BF16)
    wait(wall_t.at[pl.ds(0, 3 * DH)], in_sem.at[3])
    wall[...] = wall_t[...].T
    wait(wg.at[me], in_sem.at[4])

    twin = tid(y, x, co)

    def tell_twin(sem):
        pl.semaphore_signal(sem, inc=1, device_id=(tm, twin), device_id_type=MESH)

    @pl.when(c == 0)
    def _():
        pl.semaphore_wait(barrier, TOK - 1)
        tell_twin(tok_ready)

    @pl.when(c == 1)
    def _():
        pl.semaphore_wait(tok_ready, 1)

    halves = ((0, 32), (32, 32))
    quarters = ((0, 16), (16, 16), (32, 16), (48, 16))
    whole = (0, 64)
    right, left, over = tid(y, xp, c), tid(y, xm, c), tid(yo, x, c)
    row_of, column_of = (y, yo), {"L": xm, "R": xp, "F": xa, "0": x}

    class Gather:
        def __init__(self, buf, send_sem, recv_sem, one_twin):
            self.buf, self.send_sem, self.recv_sem, self.index, self.one_twin = buf, send_sem, recv_sem, {}, one_twin

        def sem(self, *key):
            return self.recv_sem.at[self.index.setdefault(key, len(self.index))]

        def part(self, block, piece):
            return self.buf.at[block, pl.ds(piece[0], piece[1])]

        def send(self, block, piece, to, *key, group=None):
            part = self.part(block, piece)
            remote(part, part, self.send_sem, self.sem(*key), tm if group is None else group, to).start()

        def wait(self, block, piece, *key):
            wait(self.part(block, piece), self.sem(*key))

        def to_twin(self, block, piece, row, place):
            key = ("twin",) if self.one_twin else ("twin", row, place)
            self.send(block, piece, twin, *key)

        def wait_twin(self, row, place):
            self.wait(tid(row_of[row], column_of[place], co), whole, "twin", row, place)

        def own_x(self, piece):
            self.send(me, piece, right, 0, "L", piece)
            self.send(me, piece, left, 0, "R", piece)

        def relay_even(self, row, even):
            from_left, from_right = tid(row_of[row], xm, c), tid(row_of[row], xp, c)
            self.wait(from_left, even, row, "L", even)
            self.send(from_left, even, right, row, "F")
            self.wait(from_right, even, row, "R", even)
            self.to_twin(from_left, even, row, "L")
            self.to_twin(from_right, even, row, "R")

        def relay_odd(self, row, odd):
            from_left, from_right = tid(row_of[row], xm, c), tid(row_of[row], xp, c)
            self.wait(from_right, odd, row, "R", odd)
            self.send(from_right, odd, left, row, "F")
            self.wait(from_left, odd, row, "L", odd)
            self.to_twin(from_left, odd, row, "L")
            self.to_twin(from_right, odd, row, "R")

        def relay(self, row, pieces):
            for even, odd in zip(pieces[::2], pieces[1::2]):
                self.relay_even(row, even)
                self.relay_odd(row, odd)

        def spread_over(self, piece):
            self.send(over, piece, right, 1, "L", piece)
            self.send(over, piece, left, 1, "R", piece)
            self.to_twin(over, piece, 1, "0")

        def far(self, row):
            block = tid(row_of[row], xa, c)
            self.wait(block, whole, row, "F")
            self.to_twin(block, whole, row, "F")

    tok = Gather(xg, tok_send, tok_recv, False)
    out = Gather(wg, out_send, out_recv, True)

    def chip_rows(row, place):
        chip = row_of[row] * 4 + column_of[place]
        return chip, pl.ds(chip * 128, 128)

    def slot(row, place):
        return pl.ds((7 - row * 4 - "0LRF".index(place)) * 128, 128)

    def project(row, place):
        chip, rows = chip_rows(row, place)
        tokens = xg[pl.ds(chip * 2, 2)].reshape(128, D)
        made = jnp.dot(tokens, wall[...], preferred_element_type=F32).astype(BF16)
        kv[rows] = made[:, 0:128]
        qb[rows] = made[:, 128:256]

        @pl.when(tm == 0)
        def _():
            keyval[slot(row, place)] = made[:, 0:128]

    def pass_on(row, place):
        chip, rows = chip_rows(row, place)

        to = 7 - row * 4 - "0LRF".index(place)
        if to > 0:
            @pl.when(tm == 0)
            def _():
                remote(keyval.at[slot(row, place)], keyval.at[slot(row, place)], down_send, down_recv, to, me).start()

        @pl.when((tm < TM - 1) & (tm >= (1 if to == 1 else 0)))
        def _():
            remote(kv.at[rows], keyval.at[pl.ds(1024 + chip * 128, 128)], kv_send, kv_recv,
                   jnp.minimum(tm + 1, TM - 1), me).start()

    def over_in(piece):
        tok.wait(over, piece, "over", piece)
        tok.spread_over(piece)

    part = pl.ds(z * 128, 128)

    def anchor(to, recv):
        remote(keyval.at[part], keyval.at[part], anchor_send, recv, to, me).start()

    def anchor_down():
        for k in (3, 2, 1):
            anchor(k * 8 + z, down_recv)

    def anchor_along():
        def one(to):
            @pl.when((to != z) & (y_lo + to > 0))
            def _():
                anchor(y_lo * 8 + to, anchor_recv)

        each(0, 8, one)

    def own_over(i):
        tok.send(me, quarters[i], over, "over", quarters[i])

    own_over(0)
    tok.own_x(halves[0])
    own_over(1)
    tok.own_x(halves[1])
    own_over(2)
    tok.to_twin(me, whole, 0, "0")
    own_over(3)
    tok.wait_twin(0, "0")
    project(0, "0")

    tok.relay_even(0, halves[0])
    over_in(quarters[0])
    tok.relay_odd(0, halves[1])
    over_in(quarters[1])
    for place in ("L", "R"):
        tok.wait_twin(0, place)
        project(0, place)
    over_in(quarters[2])
    over_in(quarters[3])

    @pl.when(c == 1)
    def _():
        pl.semaphore_wait(barrier, 25)
        tell_twin(tm_ready)

    @pl.when(c == 0)
    def _():
        pl.semaphore_wait(tm_ready, 1)

    for place in ("0", "L", "R"):
        pass_on(0, place)
    mine, theirs = (32 * (z % 2), 32), (32 - 32 * (z % 2), 32)
    out.send(me, mine, over, "over")
    tok.far(0)
    tok.relay(1, quarters[:2])
    tok.wait_twin(0, "F")
    project(0, "F")
    pass_on(0, "F")
    late = z >= 4

    def forward_part():
        wait(keyval.at[part], down_recv)
        anchor_down()
        anchor_along()

    @pl.when((tm < 8) & late)
    def _():
        forward_part()

    tok.relay(1, quarters[2:])
    out.own_x(halves[0])
    out.own_x(halves[1])
    out.to_twin(me, whole, 0, "0")
    for place in ("0", "L", "R"):
        tok.wait_twin(1, place)
        project(1, place)
        pass_on(1, place)
    out.wait(over, mine, "over")
    out.send(over, mine, me, "next", group=tm + 1 - 2 * (z % 2))

    @pl.when((tm > 0) & (tm < 8) & ~late)
    def _():
        forward_part()

    @pl.when((tm >= 8) & late)
    def _():
        wait(keyval.at[part], down_recv)
        anchor_along()

    tok.far(1)
    tok.wait_twin(1, "F")
    project(1, "F")
    pass_on(1, "F")
    out.relay(0, halves)

    @pl.when(tm == 0)
    def _():
        keyval[1024:2048] = kv[...]
        anchor_down()
        anchor_along()

    @pl.when((tm >= 8) & ~late)
    def _():
        wait(keyval.at[part], down_recv)
        anchor_along()

    out.wait(over, theirs, "next")
    for half in halves:
        out.spread_over(half)

    anchor_first = z == 0
    first_keys = pl.ds(jnp.where(anchor_first, 0, 1024), 1024)
    second_keys = pl.ds(jnp.where(anchor_first, 1024, 0), 1024)

    def wait_anchor():
        wait(keyval.at[pl.ds(0, 7 * 128)], anchor_recv)

    def wait_prev():
        @pl.when(tm == 1)
        def _():
            wait(keyval.at[pl.ds(1024, 7 * 128)], kv_recv)
            keyval[pl.ds(1024 + chip_rows(1, "R")[0] * 128, 128)] = keyval[slot(1, "R")]

        @pl.when(tm > 1)
        def _():
            wait(keyval.at[pl.ds(1024, 1024)], kv_recv)

    @pl.when(anchor_first & (tm > 0))
    def _():
        wait_anchor()

    @pl.when(z > 0)
    def _():
        wait_prev()

    low = lax.broadcasted_iota(jnp.int32, (HALF, 128), 1) < DH
    nt = (((1,), (1,)), ((), ()))

    def chunk(i):
        yy = (y + 1 + i // 2) % 2
        pp = (x // 2 + 1 + i) % 2
        return yy * 8 + pp * 4

    def attend_first(i):
        rows = pl.ds(chunk(i) * ROWS, 4 * ROWS)
        scores = lax.dot_general(qb[rows], keyval[first_keys], nt, preferred_element_type=F32)
        highest = jnp.max(scores, axis=-1, keepdims=True)
        weights = jnp.exp2((scores - highest) * EXP_SCALE)
        e_first[rows] = weights
        m_first[rows] = jnp.broadcast_to(highest, (4 * ROWS, 128))
        l_first[rows] = jnp.broadcast_to(jnp.sum(weights, axis=-1, keepdims=True), (4 * ROWS, 128))

    def attend(i):
        first = chunk(i)
        rows = pl.ds(first * ROWS, 4 * ROWS)
        scores = lax.dot_general(qb[rows], keyval[second_keys], nt, preferred_element_type=F32)
        before = m_first[rows][:, 0:1]
        highest = jnp.maximum(jnp.max(scores, axis=-1, keepdims=True), before)
        weights = jnp.exp2((scores - highest) * EXP_SCALE)
        shrink = jnp.exp2((before - highest) * EXP_SCALE)
        inverse = 1.0 / (jnp.sum(weights, axis=-1, keepdims=True) + l_first[rows][:, 0:1] * shrink)
        p_second = (weights * inverse).astype(BF16)
        p_first = (e_first[rows] * (shrink * inverse)).astype(BF16)
        mixed = jnp.dot(p_second, keyval[second_keys], preferred_element_type=F32)
        mixed = mixed + jnp.dot(p_first, keyval[first_keys], preferred_element_type=F32)
        for k in range(4):
            top = mixed[k * ROWS : k * ROWS + HALF]
            bottom = mixed[k * ROWS + HALF : (k + 1) * ROWS]
            to = first + k
            msend[to] = jnp.where(low, pltpu.roll(top, DH, 1), bottom).astype(BF16)

            @pl.when(to != me)
            def _():
                remote(msend.at[to], mg.at[me], mix_send, mix_recv, tm, to).start()

    each(0, 4, attend_first)
    out.relay(1, halves)
    out.far(0)

    @pl.when(anchor_first & (tm > 0))
    def _():
        wait_prev()

    @pl.when(z > 0)
    def _():
        wait_anchor()

    each(0, 4, attend)
    out.far(1)
    mg[me] = msend[me]

    wait(xg.at[pl.ds(0, 15)], tok_send)

    @pl.when(tm == 0)
    def _():
        wait(kv.at[pl.ds(0, 7 * 128)], down_send)
        wait(keyval.at[pl.ds(0, 10 * 128)], anchor_send)

    @pl.when((tm > 0) & (tm < 8))
    def _():
        wait(keyval.at[pl.ds(0, 9 * 128)], anchor_send)

    @pl.when(tm >= 8)
    def _():
        wait(keyval.at[pl.ds(0, 7 * 128)], anchor_send)

    @pl.when(tm == 0)
    def _():
        wait(kv.at[pl.ds(0, 7 * 128)], kv_send)

    @pl.when((tm > 0) & (tm < TM - 1))
    def _():
        wait(kv, kv_send)

    wait(mg.at[pl.ds(0, TOK - 1)], mix_recv)
    for i in range(8):
        even = mg[2 * i].astype(F32)
        odd = mg[2 * i + 1].astype(F32)
        lhs[0:HALF, i * 128 : (i + 1) * 128] = jnp.where(low, even, pltpu.roll(odd, DH, 1)).astype(BF16)
        lhs[HALF:ROWS, i * 128 : (i + 1) * 128] = jnp.where(low, pltpu.roll(even, DH, 1), odd).astype(BF16)
    wait(wg.at[pl.ds(0, 8)], out.sem("twin"))
    o_ref[0] = jnp.dot(lhs[...], wg[...].reshape(TOK * DH, D), preferred_element_type=F32).astype(BF16)
    wait(wg.at[pl.ds(0, 15)], out_send)
    wait(msend.at[pl.ds(0, TOK - 1)], mix_send)


def body(hidden_states, norm_gain, norm_bias, q_weight, k_weight, v_weight, out_weight):
    anywhere = pl.BlockSpec(memory_space=pltpu.HBM)
    vmem = pltpu.VMEM
    dma = pltpu.SemaphoreType.DMA
    return pl.pallas_call(
        kernel,
        out_shape=jax.ShapeDtypeStruct((1, ROWS, D), BF16),
        in_specs=[anywhere] * 7,
        out_specs=pl.BlockSpec(memory_space=pltpu.VMEM),
        scratch_shapes=[
            vmem((ROWS, D), BF16), vmem((D,), F32), vmem((D,), F32),
            vmem((256, D), BF16),
            vmem((D, 256), BF16),
            vmem((TOK, ROWS, D), BF16),
            vmem((TOK, ROWS, D), BF16),
            vmem((1024, 128), BF16),
            vmem((2048, 128), BF16),
            vmem((1024, 128), BF16),
            vmem((1024, 1024), F32),
            vmem((1024, 128), F32),
            vmem((1024, 128), F32),
            vmem((TOK, HALF, 128), BF16),
            vmem((TOK, HALF, 128), BF16),
            vmem((ROWS, TOK * DH), BF16),
            dma((5,)), dma, dma((26,)), dma, dma((13,)),
            dma, dma, dma, dma, dma, dma, dma, dma,
            pltpu.SemaphoreType.REGULAR, pltpu.SemaphoreType.REGULAR,
        ],
        compiler_params=pltpu.CompilerParams(
            collective_id=0, has_side_effects=True, vmem_limit_bytes=VMEM_LIMIT),
        cost_estimate=pl.CostEstimate(flops=1_200_000_000, bytes_accessed=2_000_000, transcendentals=2_000_000),
        name="cross_frame_attention",
    )(hidden_states, norm_gain, norm_bias, q_weight.T, k_weight.T, v_weight.T, out_weight)


def solution(mesh):
    return jax.shard_map(
        body,
        mesh=mesh,
        in_specs=(P("tm", "tok", None), P(), P(), P(None, "tok"), P(None, "tok"), P(None, "tok"), P("tok", None)),
        out_specs=P("tm", "tok", None),
        check_vma=False,
    )
```

```python
import functools
import math

import jax
import jax.numpy as jnp
from jax import lax
from jax.experimental import pallas as pl
from jax.experimental.pallas import tpu as pltpu
from jax.sharding import PartitionSpec as P

MESH = pl.DeviceIdType.MESH
D = 1280
DH = 64
ROWS = 64
HALF = 32
TM = 32
TOK = 16
F32 = jnp.float32
BF16 = jnp.bfloat16
VMEM_LIMIT = 63 * 2**20
EXP_SCALE = DH ** (-0.5) / math.log(2.0)


def layer_norm(states, gain, bias):
    widened = states.astype(F32)
    center = jnp.mean(widened, axis=-1, keepdims=True)
    moved = widened - center
    spread = jnp.mean(jnp.square(moved), axis=-1, keepdims=True)
    return moved * lax.rsqrt(spread + 1e-05) * gain + bias


def kernel(
    x_hbm, gain_hbm, bias_hbm, wq_hbm, wk_hbm, wv_hbm, wo_hbm, o_ref,
    x_in, gain, bias, wall_t,
    wall, xg, wg, kv, keyval, qb, e_first, m_first, l_first, e_second, m_second, l_second, msend, mg, lhs, partial,
    in_sem, tok_send, tok_recv, out_send, out_recv,
    down_send, down_recv, anchor_send, anchor_recv, kv_send, kv_recv, mix_out, mix_near, mix_far,
    tok_ready, tm_ready,
):
    tm = lax.axis_index("tm")
    y_lo, z = tm // 8, tm % 8
    me = lax.axis_index("tok")
    y, x, c = me // 8, (me // 2) % 4, me % 2
    xp, xm, xa = (x + 1) % 4, (x + 3) % 4, (x + 2) % 4
    yo, co = 1 - y, 1 - c

    def tid(yy, xx, cc):
        return yy * 8 + xx * 2 + cc

    def each(start, stop, step):
        lax.fori_loop(start, stop, lambda i, carry: (step(i), carry)[1], 0)

    def wait(ref, sem):
        pltpu.make_async_copy(ref, ref, sem).wait()

    def remote(src, dst, send_sem, recv_sem, group, to):
        return pltpu.make_async_remote_copy(
            src_ref=src, dst_ref=dst, send_sem=send_sem, recv_sem=recv_sem,
            device_id=(group, to), device_id_type=MESH)

    for i, src, dst in (
        (0, x_hbm.at[0], x_in), (1, gain_hbm, gain), (2, bias_hbm, bias),
        (3, wk_hbm, wall_t.at[pl.ds(0, DH)]), (3, wv_hbm, wall_t.at[pl.ds(DH, DH)]),
        (3, wq_hbm, wall_t.at[pl.ds(2 * DH, DH)]), (4, wo_hbm, wg.at[me]),
    ):
        pltpu.make_async_copy(src, dst, in_sem.at[i]).start()

    barrier = pltpu.get_barrier_semaphore()

    def greet(group, to):
        pl.semaphore_signal(barrier, inc=1, device_id=(group, to), device_id_type=MESH)

    @pl.when(c == 0)
    def _():
        greet(tm, me + 1)

    @pl.when(c == 1)
    def _():
        greet(tm, me - 1)

    each(1, 8, lambda i: greet(tm, (me + 2 * i) % TOK - c))
    far_side = tid(y, x, 1)
    each(1, 4, lambda i: greet((tm + 8 * i) % TM, far_side))
    each(1, 8, lambda i: greet(y_lo * 8 + (z + i) % 8, far_side))
    greet((tm + 1) % TM, far_side)
    greet((tm + TM - 1) % TM, far_side)

    wait(x_in, in_sem.at[0])
    wait(gain, in_sem.at[1])
    wait(bias, in_sem.at[2])
    normed = layer_norm(x_in[...], gain[...].reshape(1, D), bias[...].reshape(1, D))
    xg[me] = normed.astype(BF16)

    wall_t[3 * DH :] = jnp.zeros((DH, D), BF16)
    wait(wall_t.at[pl.ds(0, 3 * DH)], in_sem.at[3])
    wall[...] = wall_t[...].T
    wait(wg.at[me], in_sem.at[4])

    twin = tid(y, x, co)

    def tell_twin(sem):
        pl.semaphore_signal(sem, inc=1, device_id=(tm, twin), device_id_type=MESH)

    @pl.when(c == 0)
    def _():
        pl.semaphore_wait(barrier, TOK - 1)
        tell_twin(tok_ready)

    @pl.when(c == 1)
    def _():
        pl.semaphore_wait(tok_ready, 1)

    halves = ((0, 32), (32, 32))
    quarters = ((0, 16), (16, 16), (32, 16), (48, 16))
    whole = (0, 64)
    right, left, over = tid(y, xp, c), tid(y, xm, c), tid(yo, x, c)
    row_of, column_of = (y, yo), {"L": xm, "R": xp, "F": xa, "0": x}

    class Gather:
        def __init__(self, buf, send_sem, recv_sem, one_twin):
            self.buf, self.send_sem, self.recv_sem, self.index, self.one_twin = buf, send_sem, recv_sem, {}, one_twin

        def sem(self, *key):
            return self.recv_sem.at[self.index.setdefault(key, len(self.index))]

        def part(self, block, piece):
            return self.buf.at[block, pl.ds(piece[0], piece[1])]

        def send(self, block, piece, to, *key, group=None):
            part = self.part(block, piece)
            remote(part, part, self.send_sem, self.sem(*key), tm if group is None else group, to).start()

        def wait(self, block, piece, *key):
            wait(self.part(block, piece), self.sem(*key))

        def to_twin(self, block, piece, row, place):
            key = ("twin",) if self.one_twin else ("twin", row, place)
            self.send(block, piece, twin, *key)

        def wait_twin(self, row, place):
            self.wait(tid(row_of[row], column_of[place], co), whole, "twin", row, place)

        def own_x(self, piece):
            self.send(me, piece, right, 0, "L", piece)
            self.send(me, piece, left, 0, "R", piece)

        def relay_even(self, row, even):
            from_left, from_right = tid(row_of[row], xm, c), tid(row_of[row], xp, c)
            self.wait(from_left, even, row, "L", even)
            self.send(from_left, even, right, row, "F")
            self.wait(from_right, even, row, "R", even)
            self.to_twin(from_left, even, row, "L")
            self.to_twin(from_right, even, row, "R")

        def relay_odd(self, row, odd):
            from_left, from_right = tid(row_of[row], xm, c), tid(row_of[row], xp, c)
            self.wait(from_right, odd, row, "R", odd)
            self.send(from_right, odd, left, row, "F")
            self.wait(from_left, odd, row, "L", odd)
            self.to_twin(from_left, odd, row, "L")
            self.to_twin(from_right, odd, row, "R")

        def relay(self, row, pieces):
            for even, odd in zip(pieces[::2], pieces[1::2]):
                self.relay_even(row, even)
                self.relay_odd(row, odd)

        def spread_over(self, piece):
            self.send(over, piece, right, 1, "L", piece)
            self.send(over, piece, left, 1, "R", piece)
            self.to_twin(over, piece, 1, "0")

        def far(self, row):
            block = tid(row_of[row], xa, c)
            self.wait(block, whole, row, "F")
            self.to_twin(block, whole, row, "F")

    tok = Gather(xg, tok_send, tok_recv, False)
    out = Gather(wg, out_send, out_recv, True)

    def chip_rows(row, place):
        chip = row_of[row] * 4 + column_of[place]
        return chip, pl.ds(chip * 128, 128)

    def slot(row, place):
        return pl.ds((7 - row * 4 - "0LRF".index(place)) * 128, 128)

    def project(row, place):
        chip, rows = chip_rows(row, place)
        tokens = xg[pl.ds(chip * 2, 2)].reshape(128, D)
        made = jnp.dot(tokens, wall[...], preferred_element_type=F32).astype(BF16)
        kv[rows] = made[:, 0:128]
        qb[rows] = made[:, 128:256]

        @pl.when(tm == 0)
        def _():
            keyval[slot(row, place)] = made[:, 0:128]

    def pass_on(row, place):
        chip, rows = chip_rows(row, place)

        to = 7 - row * 4 - "0LRF".index(place)
        if to > 0:
            @pl.when(tm == 0)
            def _():
                remote(keyval.at[slot(row, place)], keyval.at[slot(row, place)], down_send, down_recv, to, me).start()

        @pl.when((tm > 0) & (tm < TM - 1))
        def _():
            remote(kv.at[rows], keyval.at[pl.ds(1024 + chip * 128, 128)], kv_send, kv_recv,
                   jnp.minimum(tm + 1, TM - 1), me).start()

    def over_in(piece):
        tok.wait(over, piece, "over", piece)
        tok.spread_over(piece)

    part = pl.ds(z * 128, 128)

    def anchor(to, recv):
        remote(keyval.at[part], keyval.at[part], anchor_send, recv, to, me).start()

    def anchor_down():
        for k in (3, 2, 1):
            anchor(k * 8 + z, down_recv)

    def anchor_along():
        def one(to):
            @pl.when((to != z) & (y_lo + to > 0))
            def _():
                anchor(y_lo * 8 + to, anchor_recv)

        each(0, 8, one)

    def own_over(i):
        tok.send(me, quarters[i], over, "over", quarters[i])

    own_over(0)
    tok.own_x(halves[0])
    own_over(1)
    tok.own_x(halves[1])
    own_over(2)
    tok.to_twin(me, whole, 0, "0")
    own_over(3)
    tok.wait_twin(0, "0")
    project(0, "0")

    tok.relay_even(0, halves[0])
    over_in(quarters[0])
    tok.relay_odd(0, halves[1])
    over_in(quarters[1])
    for place in ("L", "R"):
        tok.wait_twin(0, place)
        project(0, place)
    over_in(quarters[2])
    over_in(quarters[3])

    @pl.when(c == 1)
    def _():
        pl.semaphore_wait(barrier, 25)
        tell_twin(tm_ready)

    @pl.when(c == 0)
    def _():
        pl.semaphore_wait(tm_ready, 1)

    for place in ("0", "L", "R"):
        pass_on(0, place)
    late, last = z >= 4, z >= 5

    def forward_part():
        wait(keyval.at[part], down_recv)
        anchor_down()
        anchor_along()

    def forward_along():
        wait(keyval.at[part], down_recv)
        anchor_along()

    def own_over_out():
        for half in halves:
            out.send(me, half, over, "over", half)

    @pl.when(~last)
    def _():
        own_over_out()

    @pl.when((tm < 8) & last)
    def _():
        forward_part()

    tok.far(0)
    tok.relay(1, quarters[:2])
    tok.wait_twin(0, "F")
    project(0, "F")
    pass_on(0, "F")
    @pl.when(tm == 4)
    def _():
        forward_part()

    tok.relay(1, quarters[2:])
    out.own_x(halves[0])
    out.own_x(halves[1])
    out.to_twin(me, whole, 0, "0")
    for place in ("0", "L", "R"):
        tok.wait_twin(1, place)
        project(1, place)
        pass_on(1, place)
    @pl.when((tm > 0) & (tm < 8) & ~late)
    def _():
        forward_part()

    tok.far(1)
    tok.wait_twin(1, "F")
    project(1, "F")
    pass_on(1, "F")

    @pl.when(last)
    def _():
        own_over_out()

    out.relay(0, halves)

    @pl.when(tm == 0)
    def _():
        keyval[1024:2048] = kv[...]
        anchor_down()
        anchor_along()

    @pl.when(tm >= 8)
    def _():
        forward_along()

    for half in halves:
        out.wait(over, half, "over", half)
        out.spread_over(half)

    first_keys, second_keys = slice(1024, 2048), slice(0, 1024)

    def wait_anchor():
        wait(keyval.at[pl.ds(0, 7 * 128)], anchor_recv)

    @pl.when(tm == 1)
    def _():
        wait_anchor()
        keyval[1024:2048] = keyval[0:1024]

    @pl.when(tm > 1)
    def _():
        wait(keyval.at[pl.ds(1024, 1024)], kv_recv)

    low = lax.broadcasted_iota(jnp.int32, (HALF, 128), 1) < DH
    nt = (((1,), (1,)), ((), ()))

    def weigh(rows, count, keys, weights_ref, highest_ref, total_ref):
        scores = lax.dot_general(qb[rows], keyval[keys], nt, preferred_element_type=F32)
        highest = jnp.max(scores, axis=-1, keepdims=True)
        weights = jnp.exp2((scores - highest) * EXP_SCALE)
        weights_ref[rows] = weights
        highest_ref[rows] = jnp.broadcast_to(highest, (count, 128))
        total_ref[rows] = jnp.broadcast_to(jnp.sum(weights, axis=-1, keepdims=True), (count, 128))

    def mix(first, count):
        rows = pl.ds(first * ROWS, count * ROWS)
        top_first, top_second = m_first[rows][:, 0:1], m_second[rows][:, 0:1]
        highest = jnp.maximum(top_first, top_second)
        shrink_first = jnp.exp2((top_first - highest) * EXP_SCALE)
        shrink_second = jnp.exp2((top_second - highest) * EXP_SCALE)
        inverse = 1.0 / (l_first[rows][:, 0:1] * shrink_first + l_second[rows][:, 0:1] * shrink_second)
        p_first = (e_first[rows] * (shrink_first * inverse)).astype(BF16)
        p_second = (e_second[rows] * (shrink_second * inverse)).astype(BF16)
        mixed = jnp.dot(p_first, keyval[first_keys], preferred_element_type=F32)
        mixed = mixed + jnp.dot(p_second, keyval[second_keys], preferred_element_type=F32)
        for k in range(count):
            top = mixed[k * ROWS : k * ROWS + HALF]
            bottom = mixed[k * ROWS + HALF : (k + 1) * ROWS]
            msend[first + k] = jnp.where(low, pltpu.roll(top, DH, 1), bottom).astype(BF16)

    def mix_send(to, near):
        remote(msend.at[to], mg.at[me], mix_out, mix_near if near else mix_far, tm, to).start()

    weigh(slice(0, 1024), 1024, first_keys, e_first, m_first, l_first)
    out.relay(1, halves)
    out.far(0)

    @pl.when(tm > 1)
    def _():
        wait_anchor()

    for yy in (yo, y):
        weigh(pl.ds(yy * 8 * ROWS, 8 * ROWS), 8 * ROWS, second_keys, e_second, m_second, l_second)
        for quad in (0, 4):
            mix(yy * 8 + quad, 4)
            if yy is yo:
                each(quad, quad + 4, lambda k: mix_send(yo * 8 + k, False))
    each(1, 8, lambda k: mix_send(y * 8 + (me + k) % 8, True))
    out.far(1)
    mg[me] = msend[me]

    wait(xg.at[pl.ds(0, 15)], tok_send)

    @pl.when(tm == 0)
    def _():
        wait(keyval.at[pl.ds(0, 7 * 128)], down_send)
        wait(keyval.at[pl.ds(0, 10 * 128)], anchor_send)

    @pl.when((tm > 0) & (tm < 8))
    def _():
        wait(keyval.at[pl.ds(0, 9 * 128)], anchor_send)

    @pl.when(tm >= 8)
    def _():
        wait(keyval.at[pl.ds(0, 7 * 128)], anchor_send)

    @pl.when((tm > 0) & (tm < TM - 1))
    def _():
        wait(kv, kv_send)

    def gathered(yy):
        for i in range(4):
            even = mg[yy * 8 + 2 * i].astype(F32)
            odd = mg[yy * 8 + 2 * i + 1].astype(F32)
            lhs[0:HALF, i * 128 : (i + 1) * 128] = jnp.where(low, even, pltpu.roll(odd, DH, 1)).astype(BF16)
            lhs[HALF:ROWS, i * 128 : (i + 1) * 128] = jnp.where(low, pltpu.roll(even, DH, 1), odd).astype(BF16)
        weights = wg[pl.ds(yy * 8, 8)].reshape(8 * DH, D)
        return jnp.dot(lhs[...], weights, preferred_element_type=F32)

    wait(wg.at[pl.ds(0, 8)], out.sem("twin"))
    wait(mg.at[pl.ds(0, 7)], mix_near)
    partial[...] = gathered(y)
    wait(mg.at[pl.ds(0, 8)], mix_far)
    o_ref[0] = (partial[...] + gathered(yo)).astype(BF16)
    wait(wg.at[pl.ds(0, 15)], out_send)
    wait(msend.at[pl.ds(0, TOK - 1)], mix_out)


def body(hidden_states, norm_gain, norm_bias, q_weight, k_weight, v_weight, out_weight):
    anywhere = pl.BlockSpec(memory_space=pltpu.HBM)
    vmem = pltpu.VMEM
    dma = pltpu.SemaphoreType.DMA
    return pl.pallas_call(
        kernel,
        out_shape=jax.ShapeDtypeStruct((1, ROWS, D), BF16),
        in_specs=[anywhere] * 7,
        out_specs=pl.BlockSpec(memory_space=pltpu.VMEM),
        scratch_shapes=[
            vmem((ROWS, D), BF16), vmem((D,), F32), vmem((D,), F32),
            vmem((256, D), BF16),
            vmem((D, 256), BF16),
            vmem((TOK, ROWS, D), BF16),
            vmem((TOK, ROWS, D), BF16),
            vmem((1024, 128), BF16),
            vmem((2048, 128), BF16),
            vmem((1024, 128), BF16),
            vmem((1024, 1024), F32),
            vmem((1024, 128), F32),
            vmem((1024, 128), F32),
            vmem((1024, 1024), F32),
            vmem((1024, 128), F32),
            vmem((1024, 128), F32),
            vmem((TOK, HALF, 128), BF16),
            vmem((TOK, HALF, 128), BF16),
            vmem((ROWS, 8 * DH), BF16),
            vmem((ROWS, D), F32),
            dma((5,)), dma, dma((26,)), dma, dma((13,)),
            dma, dma, dma, dma, dma, dma, dma, dma, dma,
            pltpu.SemaphoreType.REGULAR, pltpu.SemaphoreType.REGULAR,
        ],
        compiler_params=pltpu.CompilerParams(
            collective_id=0, has_side_effects=True, vmem_limit_bytes=VMEM_LIMIT),
        cost_estimate=pl.CostEstimate(flops=1_200_000_000, bytes_accessed=2_000_000, transcendentals=2_000_000),
        name="cross_frame_attention",
    )(hidden_states, norm_gain, norm_bias, q_weight.T, k_weight.T, v_weight.T, out_weight)


def solution(mesh):
    return jax.shard_map(
        body,
        mesh=mesh,
        in_specs=(P("tm", "tok", None), P(), P(), P(None, "tok"), P(None, "tok"), P(None, "tok"), P("tok", None)),
        out_specs=P("tm", "tok", None),
        check_vma=False,
    )
```

```python
import functools
import math

import jax
import jax.numpy as jnp
from jax import lax
from jax.experimental import pallas as pl
from jax.experimental.pallas import tpu as pltpu
from jax.sharding import PartitionSpec as P

MESH = pl.DeviceIdType.MESH
D = 1280
DH = 64
ROWS = 64
HALF = 32
TM = 32
TOK = 16
F32 = jnp.float32
BF16 = jnp.bfloat16
VMEM_LIMIT = 53 * 2**20 + 2**19 + 16 * 2**14
EXP_SCALE = DH ** (-0.5) / math.log(2.0)


def layer_norm(states, gain, bias):
    widened = states.astype(F32)
    center = jnp.mean(widened, axis=-1, keepdims=True)
    moved = widened - center
    spread = jnp.mean(jnp.square(moved), axis=-1, keepdims=True)
    return moved * lax.rsqrt(spread + 1e-05) * gain + bias


def kernel(
    x_hbm, gain_hbm, bias_hbm, wq_hbm, wk_hbm, wv_hbm, wo_hbm, o_ref,
    x_in, gain, bias, wall_t,
    wall, xg, wg, kv, keyval, qb, e_first, m_first, l_first, e_second, m_second, l_second, msend, mg, lhs, partial,
    in_sem, tok_send, tok_recv, out_send, out_recv,
    down_send, down_recv, anchor_send, anchor_recv, kv_send, kv_recv, mix_out, mix_near, mix_far,
    tok_ready, tm_ready,
):
    tm = lax.axis_index("tm")
    y_lo, z = tm // 8, tm % 8
    me = lax.axis_index("tok")
    y, x, c = me // 8, (me // 2) % 4, me % 2
    xp, xm, xa = (x + 1) % 4, (x + 3) % 4, (x + 2) % 4
    yo, co = 1 - y, 1 - c

    def tid(yy, xx, cc):
        return yy * 8 + xx * 2 + cc

    def each(start, stop, step):
        lax.fori_loop(start, stop, lambda i, carry: (step(i), carry)[1], 0)

    def wait(ref, sem):
        pltpu.make_async_copy(ref, ref, sem).wait()

    def remote(src, dst, send_sem, recv_sem, group, to):
        return pltpu.make_async_remote_copy(
            src_ref=src, dst_ref=dst, send_sem=send_sem, recv_sem=recv_sem,
            device_id=(group, to), device_id_type=MESH)

    for i, src, dst in (
        (0, x_hbm.at[0], x_in), (1, gain_hbm, gain), (2, bias_hbm, bias),
        (3, wk_hbm, wall_t.at[pl.ds(0, DH)]), (3, wv_hbm, wall_t.at[pl.ds(DH, DH)]),
        (3, wq_hbm, wall_t.at[pl.ds(2 * DH, DH)]), (4, wo_hbm, wg.at[me]),
    ):
        pltpu.make_async_copy(src, dst, in_sem.at[i]).start()

    barrier = pltpu.get_barrier_semaphore()

    def greet(group, to):
        pl.semaphore_signal(barrier, inc=1, device_id=(group, to), device_id_type=MESH)

    @pl.when(c == 0)
    def _():
        greet(tm, me + 1)

    @pl.when(c == 1)
    def _():
        greet(tm, me - 1)

    each(1, 8, lambda i: greet(tm, (me + 2 * i) % TOK - c))
    far_side = tid(y, x, 1)
    each(1, 4, lambda i: greet((tm + 8 * i) % TM, far_side))
    each(1, 8, lambda i: greet(y_lo * 8 + (z + i) % 8, far_side))
    greet((tm + 1) % TM, far_side)
    greet((tm + TM - 1) % TM, far_side)

    wait(x_in, in_sem.at[0])
    wait(gain, in_sem.at[1])
    wait(bias, in_sem.at[2])
    normed = layer_norm(x_in[...], gain[...].reshape(1, D), bias[...].reshape(1, D))
    xg[me] = normed.astype(BF16)

    wall_t[3 * DH :] = jnp.zeros((DH, D), BF16)
    wait(wall_t.at[pl.ds(0, 3 * DH)], in_sem.at[3])
    wall[...] = wall_t[...].T
    wait(wg.at[me], in_sem.at[4])

    twin = tid(y, x, co)

    def tell_twin(sem):
        pl.semaphore_signal(sem, inc=1, device_id=(tm, twin), device_id_type=MESH)

    @pl.when(c == 0)
    def _():
        pl.semaphore_wait(barrier, TOK - 1)
        tell_twin(tok_ready)

    @pl.when(c == 1)
    def _():
        pl.semaphore_wait(tok_ready, 1)

    halves = ((0, 32), (32, 32))
    quarters = ((0, 16), (16, 16), (32, 16), (48, 16))
    whole = (0, 64)
    right, left, over = tid(y, xp, c), tid(y, xm, c), tid(yo, x, c)
    row_of, column_of = (y, yo), {"L": xm, "R": xp, "F": xa, "0": x}

    class Gather:
        def __init__(self, buf, send_sem, recv_sem, one_twin):
            self.buf, self.send_sem, self.recv_sem, self.index, self.one_twin = buf, send_sem, recv_sem, {}, one_twin

        def sem(self, *key):
            return self.recv_sem.at[self.index.setdefault(key, len(self.index))]

        def part(self, block, piece):
            return self.buf.at[block, pl.ds(piece[0], piece[1])]

        def send(self, block, piece, to, *key, group=None):
            part = self.part(block, piece)
            remote(part, part, self.send_sem, self.sem(*key), tm if group is None else group, to).start()

        def wait(self, block, piece, *key):
            wait(self.part(block, piece), self.sem(*key))

        def to_twin(self, block, piece, row, place):
            key = ("twin",) if self.one_twin else ("twin", row, place)
            self.send(block, piece, twin, *key)

        def wait_twin(self, row, place):
            self.wait(tid(row_of[row], column_of[place], co), whole, "twin", row, place)

        def own_x(self, piece):
            self.send(me, piece, right, 0, "L", piece)
            self.send(me, piece, left, 0, "R", piece)

        def relay_even(self, row, even):
            from_left, from_right = tid(row_of[row], xm, c), tid(row_of[row], xp, c)
            self.wait(from_left, even, row, "L", even)
            self.send(from_left, even, right, row, "F")
            self.wait(from_right, even, row, "R", even)
            self.to_twin(from_left, even, row, "L")
            self.to_twin(from_right, even, row, "R")

        def relay_odd(self, row, odd):
            from_left, from_right = tid(row_of[row], xm, c), tid(row_of[row], xp, c)
            self.wait(from_right, odd, row, "R", odd)
            self.send(from_right, odd, left, row, "F")
            self.wait(from_left, odd, row, "L", odd)
            self.to_twin(from_left, odd, row, "L")
            self.to_twin(from_right, odd, row, "R")

        def relay(self, row, pieces):
            for even, odd in zip(pieces[::2], pieces[1::2]):
                self.relay_even(row, even)
                self.relay_odd(row, odd)

        def spread_over(self, piece):
            self.send(over, piece, right, 1, "L", piece)
            self.send(over, piece, left, 1, "R", piece)
            self.to_twin(over, piece, 1, "0")

        def far(self, row):
            block = tid(row_of[row], xa, c)
            self.wait(block, whole, row, "F")
            self.to_twin(block, whole, row, "F")

    tok = Gather(xg, tok_send, tok_recv, False)
    out = Gather(wg, out_send, out_recv, True)

    def chip_rows(row, place):
        chip = row_of[row] * 4 + column_of[place]
        return chip, pl.ds(chip * 128, 128)

    def slot(row, place):
        return pl.ds((7 - row * 4 - "0LRF".index(place)) * 128, 128)

    def project(row, place):
        chip, rows = chip_rows(row, place)
        tokens = xg[pl.ds(chip * 2, 2)].reshape(128, D)
        made = jnp.dot(tokens, wall[...], preferred_element_type=F32).astype(BF16)
        kv[rows] = made[:, 0:128]
        qb[rows] = made[:, 128:256]

        @pl.when(tm == 0)
        def _():
            keyval[slot(row, place)] = made[:, 0:128]

    def pass_on(row, place):
        chip, rows = chip_rows(row, place)

        to = 7 - row * 4 - "0LRF".index(place)
        if to > 0:
            @pl.when(tm == 0)
            def _():
                remote(keyval.at[slot(row, place)], keyval.at[slot(row, place)], down_send, down_recv, to, me).start()

        @pl.when((tm > 0) & (tm < TM - 1))
        def _():
            remote(kv.at[rows], keyval.at[pl.ds(1024 + chip * 128, 128)], kv_send, kv_recv,
                   jnp.minimum(tm + 1, TM - 1), me).start()

    def over_in(piece):
        tok.wait(over, piece, "over", piece)
        tok.spread_over(piece)

    part = pl.ds(z * 128, 128)

    def anchor(to, recv):
        remote(keyval.at[part], keyval.at[part], anchor_send, recv, to, me).start()

    def anchor_down():
        for k in (3, 2, 1):
            anchor(k * 8 + z, down_recv)

    def anchor_along():
        def one(to):
            @pl.when((to != z) & (y_lo + to > 0))
            def _():
                anchor(y_lo * 8 + to, anchor_recv)

        each(0, 8, one)

    def own_over(i):
        tok.send(me, quarters[i], over, "over", quarters[i])

    own_over(0)
    tok.own_x(halves[0])
    own_over(1)
    tok.own_x(halves[1])
    own_over(2)
    tok.to_twin(me, whole, 0, "0")
    own_over(3)
    tok.wait_twin(0, "0")
    project(0, "0")

    tok.relay_even(0, halves[0])
    over_in(quarters[0])
    tok.relay_odd(0, halves[1])
    over_in(quarters[1])
    for place in ("L", "R"):
        tok.wait_twin(0, place)
        project(0, place)
    over_in(quarters[2])
    over_in(quarters[3])

    @pl.when(c == 1)
    def _():
        pl.semaphore_wait(barrier, 25)
        tell_twin(tm_ready)

    @pl.when(c == 0)
    def _():
        pl.semaphore_wait(tm_ready, 1)

    for place in ("0", "L", "R"):
        pass_on(0, place)
    late, last = z >= 4, z >= 5

    def forward_part():
        wait(keyval.at[part], down_recv)
        anchor_down()
        anchor_along()

    def forward_along():
        wait(keyval.at[part], down_recv)
        anchor_along()

    def own_over_out():
        for half in halves:
            out.send(me, half, over, "over", half)

    @pl.when(~last)
    def _():
        own_over_out()

    @pl.when((tm < 8) & last)
    def _():
        forward_part()

    tok.far(0)
    tok.relay(1, quarters[:2])
    tok.wait_twin(0, "F")
    project(0, "F")
    pass_on(0, "F")
    @pl.when(tm == 4)
    def _():
        forward_part()

    tok.relay(1, quarters[2:])
    out.own_x(halves[0])
    out.own_x(halves[1])
    out.to_twin(me, whole, 0, "0")
    for place in ("0", "L", "R"):
        tok.wait_twin(1, place)
        project(1, place)
        pass_on(1, place)
    @pl.when((tm > 0) & (tm < 8) & ~late)
    def _():
        forward_part()

    tok.far(1)
    tok.wait_twin(1, "F")
    project(1, "F")
    pass_on(1, "F")

    @pl.when((tm >= 8) & last)
    def _():
        forward_along()

    @pl.when(last)
    def _():
        own_over_out()

    out.relay(0, halves)

    @pl.when(tm == 0)
    def _():
        keyval[1024:2048] = kv[...]
        anchor_down()
        anchor_along()

    @pl.when((tm >= 8) & ~last)
    def _():
        forward_along()

    for half in halves:
        out.wait(over, half, "over", half)
        out.spread_over(half)

    first_keys, second_keys = slice(1024, 2048), slice(0, 1024)

    def wait_anchor():
        wait(keyval.at[pl.ds(0, 7 * 128)], anchor_recv)

    @pl.when(tm == 1)
    def _():
        wait_anchor()
        keyval[1024:2048] = keyval[0:1024]

    @pl.when(tm > 1)
    def _():
        wait(keyval.at[pl.ds(1024, 1024)], kv_recv)

    low = lax.broadcasted_iota(jnp.int32, (HALF, 128), 1) < DH
    nt = (((1,), (1,)), ((), ()))

    def weigh(rows, count, keys, weights_ref, highest_ref, total_ref):
        scores = lax.dot_general(qb[rows], keyval[keys], nt, preferred_element_type=F32)
        highest = jnp.max(scores, axis=-1, keepdims=True)
        weights = jnp.exp2((scores - highest) * EXP_SCALE)
        weights_ref[rows] = weights
        highest_ref[rows] = jnp.broadcast_to(highest, (count, 128))
        total_ref[rows] = jnp.broadcast_to(jnp.sum(weights, axis=-1, keepdims=True), (count, 128))

    def mix(first, count):
        rows = pl.ds(first * ROWS, count * ROWS)
        top_first, top_second = m_first[rows][:, 0:1], m_second[rows][:, 0:1]
        highest = jnp.maximum(top_first, top_second)
        shrink_first = jnp.exp2((top_first - highest) * EXP_SCALE)
        shrink_second = jnp.exp2((top_second - highest) * EXP_SCALE)
        inverse = 1.0 / (l_first[rows][:, 0:1] * shrink_first + l_second[rows][:, 0:1] * shrink_second)
        p_first = (e_first[rows] * (shrink_first * inverse)).astype(BF16)
        p_second = (e_second[rows] * (shrink_second * inverse)).astype(BF16)
        mixed = jnp.dot(p_first, keyval[first_keys], preferred_element_type=F32)
        mixed = mixed + jnp.dot(p_second, keyval[second_keys], preferred_element_type=F32)
        for k in range(count):
            top = mixed[k * ROWS : k * ROWS + HALF]
            bottom = mixed[k * ROWS + HALF : (k + 1) * ROWS]
            msend[first + k] = jnp.where(low, pltpu.roll(top, DH, 1), bottom).astype(BF16)

    def mix_send(to, near):
        remote(msend.at[to], mg.at[me], mix_out, mix_near if near else mix_far, tm, to).start()

    weigh(slice(0, 1024), 1024, first_keys, e_first, m_first, l_first)
    out.relay(1, halves)
    out.far(0)

    @pl.when(tm > 1)
    def _():
        wait_anchor()

    for yy in (yo, y):
        weigh(pl.ds(yy * 8 * ROWS, 8 * ROWS), 8 * ROWS, second_keys, e_second, m_second, l_second)
        for quad in (0, 4):
            mix(yy * 8 + quad, 4)
            if yy is yo:
                each(quad, quad + 4, lambda k: mix_send(yo * 8 + k, False))
    each(1, 8, lambda k: mix_send(y * 8 + (me + k) % 8, True))
    out.far(1)
    mg[me] = msend[me]

    wait(xg.at[pl.ds(0, 15)], tok_send)

    @pl.when(tm == 0)
    def _():
        wait(keyval.at[pl.ds(0, 7 * 128)], down_send)
        wait(keyval.at[pl.ds(0, 10 * 128)], anchor_send)

    @pl.when((tm > 0) & (tm < 8))
    def _():
        wait(keyval.at[pl.ds(0, 9 * 128)], anchor_send)

    @pl.when(tm >= 8)
    def _():
        wait(keyval.at[pl.ds(0, 7 * 128)], anchor_send)

    @pl.when((tm > 0) & (tm < TM - 1))
    def _():
        wait(kv, kv_send)

    def gathered(yy):
        for i in range(4):
            even = mg[yy * 8 + 2 * i].astype(F32)
            odd = mg[yy * 8 + 2 * i + 1].astype(F32)
            lhs[0:HALF, i * 128 : (i + 1) * 128] = jnp.where(low, even, pltpu.roll(odd, DH, 1)).astype(BF16)
            lhs[HALF:ROWS, i * 128 : (i + 1) * 128] = jnp.where(low, pltpu.roll(even, DH, 1), odd).astype(BF16)
        weights = wg[pl.ds(yy * 8, 8)].reshape(8 * DH, D)
        return jnp.dot(lhs[...], weights, preferred_element_type=F32)

    wait(wg.at[pl.ds(0, 8)], out.sem("twin"))
    wait(mg.at[pl.ds(0, 7)], mix_near)
    partial[...] = gathered(y)
    wait(mg.at[pl.ds(0, 8)], mix_far)
    o_ref[0] = (partial[...] + gathered(yo)).astype(BF16)
    wait(wg.at[pl.ds(0, 15)], out_send)
    wait(msend.at[pl.ds(0, TOK - 1)], mix_out)


def body(hidden_states, norm_gain, norm_bias, q_weight, k_weight, v_weight, out_weight):
    anywhere = pl.BlockSpec(memory_space=pltpu.HBM)
    vmem = pltpu.VMEM
    dma = pltpu.SemaphoreType.DMA
    return pl.pallas_call(
        kernel,
        out_shape=jax.ShapeDtypeStruct((1, ROWS, D), BF16),
        in_specs=[anywhere] * 7,
        out_specs=pl.BlockSpec(memory_space=pltpu.VMEM),
        scratch_shapes=[
            vmem((ROWS, D), BF16), vmem((D,), F32), vmem((D,), F32),
            vmem((256, D), BF16),
            vmem((D, 256), BF16),
            vmem((TOK, ROWS, D), BF16),
            vmem((TOK, ROWS, D), BF16),
            vmem((1024, 128), BF16),
            vmem((2048, 128), BF16),
            vmem((1024, 128), BF16),
            vmem((1024, 1024), F32),
            vmem((1024, 128), F32),
            vmem((1024, 128), F32),
            vmem((1024, 1024), F32),
            vmem((1024, 128), F32),
            vmem((1024, 128), F32),
            vmem((TOK, HALF, 128), BF16),
            vmem((TOK, HALF, 128), BF16),
            vmem((ROWS, 8 * DH), BF16),
            vmem((ROWS, D), F32),
            dma((5,)), dma, dma((26,)), dma, dma((13,)),
            dma, dma, dma, dma, dma, dma, dma, dma, dma,
            pltpu.SemaphoreType.REGULAR, pltpu.SemaphoreType.REGULAR,
        ],
        compiler_params=pltpu.CompilerParams(
            collective_id=0, has_side_effects=True, vmem_limit_bytes=VMEM_LIMIT),
        cost_estimate=pl.CostEstimate(flops=1_200_000_000, bytes_accessed=2_000_000, transcendentals=2_000_000),
        name="cross_frame_attention",
    )(hidden_states, norm_gain, norm_bias, q_weight.T, k_weight.T, v_weight.T, out_weight)


def solution(mesh):
    return jax.shard_map(
        body,
        mesh=mesh,
        in_specs=(P("tm", "tok", None), P(), P(), P(None, "tok"), P(None, "tok"), P(None, "tok"), P("tok", None)),
        out_specs=P("tm", "tok", None),
        check_vma=False,
    )
```

```python
import functools
import math

import jax
import jax.numpy as jnp
from jax import lax
from jax.experimental import pallas as pl
from jax.experimental.pallas import tpu as pltpu
from jax.sharding import PartitionSpec as P

MESH = pl.DeviceIdType.MESH
D = 1280
DH = 64
ROWS = 64
HALF = 32
TM = 32
TOK = 16
F32 = jnp.float32
BF16 = jnp.bfloat16
VMEM_LIMIT = 53 * 2**20 + 2**19 + 16 * 2**14
EXP_SCALE = DH ** (-0.5) / math.log(2.0)


def layer_norm(states, gain, bias):
    widened = states.astype(F32)
    center = jnp.mean(widened, axis=-1, keepdims=True)
    moved = widened - center
    spread = jnp.mean(jnp.square(moved), axis=-1, keepdims=True)
    return moved * lax.rsqrt(spread + 1e-05) * gain + bias


def kernel(
    x_hbm, gain_hbm, bias_hbm, wq_hbm, wk_hbm, wv_hbm, wo_hbm, o_ref,
    x_in, gain, bias, wall_t,
    wall, xg, wg, kv, keyval, qb, e_first, m_first, l_first, e_second, m_second, l_second, msend, mg, lhs, partial,
    in_sem, tok_send, tok_recv, out_send, out_recv,
    down_send, down_recv, anchor_send, anchor_recv, kv_send, kv_recv, mix_out, mix_near, mix_far,
    tok_ready, tm_ready,
):
    tm = lax.axis_index("tm")
    y_lo, z = tm // 8, tm % 8
    me = lax.axis_index("tok")
    y, x, c = me // 8, (me // 2) % 4, me % 2
    xp, xm, xa = (x + 1) % 4, (x + 3) % 4, (x + 2) % 4
    yo, co = 1 - y, 1 - c

    def tid(yy, xx, cc):
        return yy * 8 + xx * 2 + cc

    def each(start, stop, step):
        lax.fori_loop(start, stop, lambda i, carry: (step(i), carry)[1], 0)

    def wait(ref, sem):
        pltpu.make_async_copy(ref, ref, sem).wait()

    def remote(src, dst, send_sem, recv_sem, group, to):
        return pltpu.make_async_remote_copy(
            src_ref=src, dst_ref=dst, send_sem=send_sem, recv_sem=recv_sem,
            device_id=(group, to), device_id_type=MESH)

    for i, src, dst in (
        (0, x_hbm.at[0], x_in), (1, gain_hbm, gain), (2, bias_hbm, bias),
        (3, wk_hbm, wall_t.at[pl.ds(0, DH)]), (3, wv_hbm, wall_t.at[pl.ds(DH, DH)]),
        (3, wq_hbm, wall_t.at[pl.ds(2 * DH, DH)]), (4, wo_hbm, wg.at[me]),
    ):
        pltpu.make_async_copy(src, dst, in_sem.at[i]).start()

    barrier = pltpu.get_barrier_semaphore()

    def greet(group, to):
        pl.semaphore_signal(barrier, inc=1, device_id=(group, to), device_id_type=MESH)

    @pl.when(c == 0)
    def _():
        greet(tm, me + 1)

    @pl.when(c == 1)
    def _():
        greet(tm, me - 1)

    each(1, 8, lambda i: greet(tm, (me + 2 * i) % TOK - c))
    far_side = tid(y, x, 1)
    each(1, 4, lambda i: greet((tm + 8 * i) % TM, far_side))
    each(1, 8, lambda i: greet(y_lo * 8 + (z + i) % 8, far_side))
    greet((tm + 1) % TM, far_side)
    greet((tm + TM - 1) % TM, far_side)

    wait(x_in, in_sem.at[0])
    wait(gain, in_sem.at[1])
    wait(bias, in_sem.at[2])
    normed = layer_norm(x_in[...], gain[...].reshape(1, D), bias[...].reshape(1, D))
    xg[me] = normed.astype(BF16)

    wall_t[3 * DH :] = jnp.zeros((DH, D), BF16)
    wait(wall_t.at[pl.ds(0, 3 * DH)], in_sem.at[3])
    wall[...] = wall_t[...].T
    wait(wg.at[me], in_sem.at[4])

    twin = tid(y, x, co)

    def tell_twin(sem):
        pl.semaphore_signal(sem, inc=1, device_id=(tm, twin), device_id_type=MESH)

    @pl.when(c == 0)
    def _():
        pl.semaphore_wait(barrier, TOK - 1)
        tell_twin(tok_ready)

    @pl.when(c == 1)
    def _():
        pl.semaphore_wait(tok_ready, 1)

    halves = ((0, 32), (32, 32))
    quarters = ((0, 16), (16, 16), (32, 16), (48, 16))
    whole = (0, 64)
    right, left, over = tid(y, xp, c), tid(y, xm, c), tid(yo, x, c)
    row_of, column_of = (y, yo), {"L": xm, "R": xp, "F": xa, "0": x}

    class Gather:
        def __init__(self, buf, send_sem, recv_sem, one_twin):
            self.buf, self.send_sem, self.recv_sem, self.index, self.one_twin = buf, send_sem, recv_sem, {}, one_twin

        def sem(self, *key):
            return self.recv_sem.at[self.index.setdefault(key, len(self.index))]

        def part(self, block, piece):
            return self.buf.at[block, pl.ds(piece[0], piece[1])]

        def send(self, block, piece, to, *key, group=None):
            part = self.part(block, piece)
            remote(part, part, self.send_sem, self.sem(*key), tm if group is None else group, to).start()

        def wait(self, block, piece, *key):
            wait(self.part(block, piece), self.sem(*key))

        def to_twin(self, block, piece, row, place):
            key = ("twin",) if self.one_twin else ("twin", row, place)
            self.send(block, piece, twin, *key)

        def wait_twin(self, row, place):
            self.wait(tid(row_of[row], column_of[place], co), whole, "twin", row, place)

        def own_x(self, piece):
            self.send(me, piece, right, 0, "L", piece)
            self.send(me, piece, left, 0, "R", piece)

        def relay_even(self, row, even):
            from_left, from_right = tid(row_of[row], xm, c), tid(row_of[row], xp, c)
            self.wait(from_left, even, row, "L", even)
            self.send(from_left, even, right, row, "F")
            self.wait(from_right, even, row, "R", even)
            self.to_twin(from_left, even, row, "L")
            self.to_twin(from_right, even, row, "R")

        def relay_odd(self, row, odd):
            from_left, from_right = tid(row_of[row], xm, c), tid(row_of[row], xp, c)
            self.wait(from_right, odd, row, "R", odd)
            self.send(from_right, odd, left, row, "F")
            self.wait(from_left, odd, row, "L", odd)
            self.to_twin(from_left, odd, row, "L")
            self.to_twin(from_right, odd, row, "R")

        def relay(self, row, pieces):
            for even, odd in zip(pieces[::2], pieces[1::2]):
                self.relay_even(row, even)
                self.relay_odd(row, odd)

        def spread_over(self, piece):
            self.send(over, piece, right, 1, "L", piece)
            self.send(over, piece, left, 1, "R", piece)
            self.to_twin(over, piece, 1, "0")

        def far(self, row):
            block = tid(row_of[row], xa, c)
            self.wait(block, whole, row, "F")
            self.to_twin(block, whole, row, "F")

    tok = Gather(xg, tok_send, tok_recv, False)
    out = Gather(wg, out_send, out_recv, True)

    def chip_rows(row, place):
        chip = row_of[row] * 4 + column_of[place]
        return chip, pl.ds(chip * 128, 128)

    def slot(row, place):
        return pl.ds((7 - row * 4 - "0LRF".index(place)) * 128, 128)

    def project(row, place):
        chip, rows = chip_rows(row, place)
        tokens = xg[pl.ds(chip * 2, 2)].reshape(128, D)
        made = jnp.dot(tokens, wall[...], preferred_element_type=F32).astype(BF16)
        kv[rows] = made[:, 0:128]
        qb[rows] = made[:, 128:256]

        @pl.when(tm == 0)
        def _():
            keyval[slot(row, place)] = made[:, 0:128]

    def pass_on(row, place):
        chip, rows = chip_rows(row, place)

        to = 7 - row * 4 - "0LRF".index(place)
        if to > 0:
            @pl.when(tm == 0)
            def _():
                remote(keyval.at[slot(row, place)], keyval.at[slot(row, place)], down_send, down_recv, to, me).start()

        @pl.when((tm > 0) & (tm < TM - 1))
        def _():
            remote(kv.at[rows], keyval.at[pl.ds(1024 + chip * 128, 128)], kv_send, kv_recv,
                   jnp.minimum(tm + 1, TM - 1), me).start()

    def over_in(piece):
        tok.wait(over, piece, "over", piece)
        tok.spread_over(piece)

    part = pl.ds(z * 128, 128)

    def anchor(to, recv):
        remote(keyval.at[part], keyval.at[part], anchor_send, recv, to, me).start()

    def anchor_down():
        for k in (3, 2, 1):
            anchor(k * 8 + z, down_recv)

    def anchor_along():
        def one(to):
            @pl.when((to != z) & (y_lo + to > 0))
            def _():
                anchor(y_lo * 8 + to, anchor_recv)

        each(0, 8, one)

    def own_over(i):
        tok.send(me, quarters[i], over, "over", quarters[i])

    own_over(0)
    tok.own_x(halves[0])
    own_over(1)
    tok.own_x(halves[1])
    own_over(2)
    tok.to_twin(me, whole, 0, "0")
    own_over(3)
    tok.wait_twin(0, "0")
    project(0, "0")

    tok.relay_even(0, halves[0])
    over_in(quarters[0])
    tok.relay_odd(0, halves[1])
    over_in(quarters[1])
    for place in ("L", "R"):
        tok.wait_twin(0, place)
        project(0, place)
    over_in(quarters[2])
    over_in(quarters[3])

    @pl.when(c == 1)
    def _():
        pl.semaphore_wait(barrier, 25)
        tell_twin(tm_ready)

    @pl.when(c == 0)
    def _():
        pl.semaphore_wait(tm_ready, 1)

    for place in ("0", "L", "R"):
        pass_on(0, place)
    late, last = z >= 4, z >= 5

    def forward_part():
        wait(keyval.at[part], down_recv)
        anchor_down()
        anchor_along()

    def forward_along():
        wait(keyval.at[part], down_recv)
        anchor_along()

    def own_over_out():
        for half in halves:
            out.send(me, half, over, "over", half)

    @pl.when(~last)
    def _():
        own_over_out()

    @pl.when((tm < 8) & last)
    def _():
        forward_part()

    tok.far(0)
    tok.relay(1, quarters[:2])
    tok.wait_twin(0, "F")
    project(0, "F")
    pass_on(0, "F")
    @pl.when(tm == 4)
    def _():
        forward_part()

    tok.relay(1, quarters[2:])
    out.own_x(halves[0])
    out.own_x(halves[1])
    out.to_twin(me, whole, 0, "0")
    for place in ("0", "L", "R"):
        tok.wait_twin(1, place)
        project(1, place)
        pass_on(1, place)
    @pl.when((tm > 0) & (tm < 8) & ~late)
    def _():
        forward_part()

    tok.far(1)
    tok.wait_twin(1, "F")
    project(1, "F")
    pass_on(1, "F")

    @pl.when((tm >= 8) & last)
    def _():
        forward_along()

    @pl.when(last)
    def _():
        own_over_out()

    out.relay(0, halves)

    @pl.when(tm == 0)
    def _():
        keyval[1024:2048] = kv[...]
        anchor_down()
        anchor_along()

    @pl.when((tm >= 8) & ~last)
    def _():
        forward_along()

    for half in halves:
        out.wait(over, half, "over", half)
        out.spread_over(half)

    first_keys, second_keys = slice(1024, 2048), slice(0, 1024)

    def wait_anchor():
        wait(keyval.at[pl.ds(0, 7 * 128)], anchor_recv)

    @pl.when(tm == 1)
    def _():
        wait_anchor()
        keyval[1024:2048] = keyval[0:1024]

    @pl.when(tm > 1)
    def _():
        wait(keyval.at[pl.ds(1024, 1024)], kv_recv)

    low = lax.broadcasted_iota(jnp.int32, (HALF, 128), 1) < DH
    nt = (((1,), (1,)), ((), ()))

    def weigh(rows, count, keys, weights_ref, highest_ref, total_ref):
        scores = lax.dot_general(qb[rows], keyval[keys], nt, preferred_element_type=F32)
        highest = jnp.max(scores, axis=-1, keepdims=True)
        weights = jnp.exp2((scores - highest) * EXP_SCALE)
        weights_ref[rows] = weights
        highest_ref[rows] = jnp.broadcast_to(highest, (count, 128))
        total_ref[rows] = jnp.broadcast_to(jnp.sum(weights, axis=-1, keepdims=True), (count, 128))

    def mix(first, count):
        rows = pl.ds(first * ROWS, count * ROWS)
        top_first, top_second = m_first[rows][:, 0:1], m_second[rows][:, 0:1]
        highest = jnp.maximum(top_first, top_second)
        shrink_first = jnp.exp2((top_first - highest) * EXP_SCALE)
        shrink_second = jnp.exp2((top_second - highest) * EXP_SCALE)
        inverse = 1.0 / (l_first[rows][:, 0:1] * shrink_first + l_second[rows][:, 0:1] * shrink_second)
        p_first = (e_first[rows] * (shrink_first * inverse)).astype(BF16)
        p_second = (e_second[rows] * (shrink_second * inverse)).astype(BF16)
        mixed = jnp.dot(p_first, keyval[first_keys], preferred_element_type=F32)
        mixed = mixed + jnp.dot(p_second, keyval[second_keys], preferred_element_type=F32)
        for k in range(count):
            top = mixed[k * ROWS : k * ROWS + HALF]
            bottom = mixed[k * ROWS + HALF : (k + 1) * ROWS]
            msend[first + k] = jnp.where(low, pltpu.roll(top, DH, 1), bottom).astype(BF16)

    def mix_send(to, near):
        remote(msend.at[to], mg.at[me], mix_out, mix_near if near else mix_far, tm, to).start()

    def near_send(k):
        @pl.when(y * 8 + k != me)
        def _():
            mix_send(y * 8 + k, True)

    weigh(slice(0, 1024), 1024, first_keys, e_first, m_first, l_first)
    out.relay(1, halves)
    out.far(0)

    @pl.when(tm > 1)
    def _():
        wait_anchor()

    for yy in (yo, y):
        weigh(pl.ds(yy * 8 * ROWS, 8 * ROWS), 8 * ROWS, second_keys, e_second, m_second, l_second)
        for quad in (0, 4):
            mix(yy * 8 + quad, 4)
            if yy is yo:
                each(quad, quad + 4, lambda k: mix_send(yo * 8 + k, False))
            else:
                each(quad, quad + 4, near_send)
    out.far(1)
    mg[me] = msend[me]

    wait(xg.at[pl.ds(0, 15)], tok_send)

    @pl.when(tm == 0)
    def _():
        wait(keyval.at[pl.ds(0, 7 * 128)], down_send)
        wait(keyval.at[pl.ds(0, 10 * 128)], anchor_send)

    @pl.when((tm > 0) & (tm < 8))
    def _():
        wait(keyval.at[pl.ds(0, 9 * 128)], anchor_send)

    @pl.when(tm >= 8)
    def _():
        wait(keyval.at[pl.ds(0, 7 * 128)], anchor_send)

    @pl.when((tm > 0) & (tm < TM - 1))
    def _():
        wait(kv, kv_send)

    def gathered(yy):
        for i in range(4):
            even = mg[yy * 8 + 2 * i].astype(F32)
            odd = mg[yy * 8 + 2 * i + 1].astype(F32)
            lhs[0:HALF, i * 128 : (i + 1) * 128] = jnp.where(low, even, pltpu.roll(odd, DH, 1)).astype(BF16)
            lhs[HALF:ROWS, i * 128 : (i + 1) * 128] = jnp.where(low, pltpu.roll(even, DH, 1), odd).astype(BF16)
        weights = wg[pl.ds(yy * 8, 8)].reshape(8 * DH, D)
        return jnp.dot(lhs[...], weights, preferred_element_type=F32)

    wait(wg.at[pl.ds(0, 8)], out.sem("twin"))
    wait(mg.at[pl.ds(0, 7)], mix_near)
    partial[...] = gathered(y)
    wait(mg.at[pl.ds(0, 8)], mix_far)
    o_ref[0] = (partial[...] + gathered(yo)).astype(BF16)
    wait(wg.at[pl.ds(0, 15)], out_send)
    wait(msend.at[pl.ds(0, TOK - 1)], mix_out)


def body(hidden_states, norm_gain, norm_bias, q_weight, k_weight, v_weight, out_weight):
    anywhere = pl.BlockSpec(memory_space=pltpu.HBM)
    vmem = pltpu.VMEM
    dma = pltpu.SemaphoreType.DMA
    return pl.pallas_call(
        kernel,
        out_shape=jax.ShapeDtypeStruct((1, ROWS, D), BF16),
        in_specs=[anywhere] * 7,
        out_specs=pl.BlockSpec(memory_space=pltpu.VMEM),
        scratch_shapes=[
            vmem((ROWS, D), BF16), vmem((D,), F32), vmem((D,), F32),
            vmem((256, D), BF16),
            vmem((D, 256), BF16),
            vmem((TOK, ROWS, D), BF16),
            vmem((TOK, ROWS, D), BF16),
            vmem((1024, 128), BF16),
            vmem((2048, 128), BF16),
            vmem((1024, 128), BF16),
            vmem((1024, 1024), F32),
            vmem((1024, 128), F32),
            vmem((1024, 128), F32),
            vmem((1024, 1024), F32),
            vmem((1024, 128), F32),
            vmem((1024, 128), F32),
            vmem((TOK, HALF, 128), BF16),
            vmem((TOK, HALF, 128), BF16),
            vmem((ROWS, 8 * DH), BF16),
            vmem((ROWS, D), F32),
            dma((5,)), dma, dma((26,)), dma, dma((13,)),
            dma, dma, dma, dma, dma, dma, dma, dma, dma,
            pltpu.SemaphoreType.REGULAR, pltpu.SemaphoreType.REGULAR,
        ],
        compiler_params=pltpu.CompilerParams(
            collective_id=0, has_side_effects=True, vmem_limit_bytes=VMEM_LIMIT),
        cost_estimate=pl.CostEstimate(flops=1_200_000_000, bytes_accessed=2_000_000, transcendentals=2_000_000),
        name="cross_frame_attention",
    )(hidden_states, norm_gain, norm_bias, q_weight.T, k_weight.T, v_weight.T, out_weight)


def solution(mesh):
    return jax.shard_map(
        body,
        mesh=mesh,
        in_specs=(P("tm", "tok", None), P(), P(), P(None, "tok"), P(None, "tok"), P(None, "tok"), P("tok", None)),
        out_specs=P("tm", "tok", None),
        check_vma=False,
    )
```
